32 devices in a mesh: cell: 8 (over z, x), net: 4 (over y, core).
Axes of the slice: x: 2, y: 2, z: 4, core: 2. Of those that a mesh axis runs over, the one named last changes fastest.
Arguments:
- cell_feat: bfloat16 [4096, 256], P('cell'), may hold values from -6 to 6
- out_grad: bfloat16 [4096, 256], P('cell'), may hold values from -6 to 6
- w_in: bfloat16 [256, 1024], replicated, may hold values from -0.25 to 0.25
- w_net: bfloat16 [256, 1024], replicated, may hold values from -0.25 to 0.25
- bias: float32 [1024], replicated, may hold values from -3 to 3
- w_out: bfloat16 [1024, 256], replicated, may hold values from -0.1875 to 0.1875
- send_idx: int32 [8, 8, 16], P('cell'), may hold values from 0 to 511
- pin_net: int32 [8, 4, 2, 512], P('cell', 'net'), may hold values from 0 to 127
- pin_ref: int32 [8, 4, 2, 512], P('cell', 'net'), may hold values from 0 to 639
- block_count: int32 [8, 4], P('cell', 'net'), may hold values from 1 to 2, as said below
Outputs:
- updated: bfloat16 [4096, 256], P(('cell', 'net'))
- cell_grad: bfloat16 [4096, 256], P(('cell', 'net'))
- grad_in: float32 [256, 1024], replicated
- grad_net: float32 [256, 1024], replicated
- grad_bias: float32 [1024], replicated
- grad_out: float32 [1024, 256], replicated
The draws below stay inside these ranges and needn't reach their ends.
Inputs may be any that keep to these rules, and one draw needn't show every extreme that they name: `block_count`: in each partition exactly one device of the net axis holds 2 live blocks; the others hold exactly 1.
All inputs are finite; a program needn't handle non-finite values.
Results may differ from the reference program's by a relative error of at most 0.0034.
Values may be sent and summed in bfloat16 or wider, within the bound.
No kernel may reach another device: no remote copies, remote signals or barrier semaphores. Data moves between devices by JAX's collectives and lax.ppermute only.
A program may use at most 64 MiB of HBM per device.

```python
import jax
import jax.numpy as jnp
from jax import lax

F = 256
H = 1024
NETS_BLK = 128
P_BLK = 512
NB_MAX = 2
CELL_DEV = 512
SLOTS = 16
PARTITIONS = 8
NET_DEVS = 4
CELLS = 4096
TABLE = 640


def draw_block_count(key, part):
    light_load = jax.random.randint(jax.random.fold_in(key, 11), (PARTITIONS, NET_DEVS), 1, NB_MAX // 2 + 1)
    heavy_at = jax.random.randint(jax.random.fold_in(key, 12), (PARTITIONS,), 0, NET_DEVS)
    column = jnp.arange(NET_DEVS, dtype=jnp.int32)
    return jnp.where(column[None, :] == heavy_at[:, None], NB_MAX, light_load).astype(jnp.int32)


def set_ends(drawn, key, least, high):
    spot = [jax.random.randint(jax.random.fold_in(key, axis), (), 0, length) for axis, length in enumerate(drawn.shape)]
    widest = drawn.shape.index(max(drawn.shape))
    beside = spot[:widest] + [(spot[widest] + 1) % drawn.shape[widest]] + spot[widest + 1:]
    return drawn.at[tuple(spot)].set(least).at[tuple(beside)].set(high)


def shard_levels(key, dims, shards, low, largest):
    loudness, own = 1.0, jax.random.fold_in(key, 6)
    for axis_at, shards_of in shards:
        draws = jnp.exp(jax.random.uniform(jax.random.fold_in(own, axis_at), (shards_of,), jnp.float32, low / len(shards), largest / len(shards)))
        loudness = loudness * jnp.repeat(draws, dims[axis_at] // shards_of).reshape([-1 if axis == axis_at else 1 for axis in range(len(dims))])
    return loudness


def gaussian(rng, extent, spread, most, split=(), kind=jnp.bfloat16):
    values = spread * jax.random.normal(rng, extent, jnp.float32)
    if split:
        values = values * shard_levels(rng, extent, split, -0.22, 0.18)
    return jnp.clip(values, -most, most).astype(kind)


def setup_inputs(seed: int = 0) -> dict:
    key_of = jax.random.split(jax.random.key(seed), 11)
    cell_feat = gaussian(key_of[0], (CELLS, F), 1.0, 6.0, ((0, 8),))
    out_grad = gaussian(key_of[1], (CELLS, F), 1.0, 6.0, ((0, 8),))
    w_in = gaussian(key_of[2], (F, H), (2 * F) ** -0.5, 0.25)
    w_net = gaussian(key_of[3], (F, H), (2 * F) ** -0.5, 0.25)
    bias = gaussian(key_of[4], (H,), 0.5, 3.0, (), jnp.float32)
    w_out = gaussian(key_of[5], (H, F), H ** -0.5, 0.1875)
    send_idx = set_ends(jax.random.randint(key_of[6], (PARTITIONS, PARTITIONS, SLOTS), 0, CELL_DEV), jax.random.fold_in(key_of[6], 1), 0, CELL_DEV - 1).astype(jnp.int32)
    pin_net = set_ends(jax.random.randint(key_of[7], (PARTITIONS, NET_DEVS, NB_MAX, P_BLK), 0, NETS_BLK), jax.random.fold_in(key_of[7], 1), 0, NETS_BLK - 1).astype(jnp.int32)
    pin_ref = set_ends(jax.random.randint(key_of[8], (PARTITIONS, NET_DEVS, NB_MAX, P_BLK), 0, TABLE), jax.random.fold_in(key_of[8], 1), 0, TABLE - 1).astype(jnp.int32)
    block_count = draw_block_count(jax.random.fold_in(key_of[10], 71), 0)
    return {"cell_feat": cell_feat, "out_grad": out_grad, "w_in": w_in, "w_net": w_net, "bias": bias, "w_out": w_out, "send_idx": send_idx, "pin_net": pin_net, "pin_ref": pin_ref, "block_count": block_count}


def block_pass(table_x, table_g, net_ids, refs, w_in, w_net, bias, w_out):
    pin_feat = table_x[refs]
    pin_grad = table_g[refs]
    onehot = (net_ids[:, None] == jnp.arange(NETS_BLK, dtype=jnp.int32)[None, :]).astype(jnp.bfloat16)
    counts = lax.optimization_barrier(jnp.sum(onehot.astype(jnp.float32), axis=0))
    inverse = 1.0 / jnp.maximum(counts, 1.0)
    net_sum = lax.dot_general(onehot, pin_feat, (((0,), (0,)), ((), ())), preferred_element_type=jnp.float32)
    net_feat = (net_sum * inverse[:, None]).astype(jnp.bfloat16)
    net_pre = jnp.dot(net_feat, w_net, preferred_element_type=jnp.float32).astype(jnp.bfloat16)
    pre_act = jnp.dot(pin_feat, w_in, preferred_element_type=jnp.float32) + jnp.dot(onehot, net_pre, preferred_element_type=jnp.float32) + bias
    hidden_full, gelu_back = jax.vjp(jax.nn.gelu, pre_act)
    hidden = hidden_full.astype(jnp.bfloat16)
    message = jnp.dot(hidden, w_out, preferred_element_type=jnp.float32)
    pulled = lax.dot_general(pin_grad, w_out, (((1,), (1,)), ((), ())), preferred_element_type=jnp.float32)
    pre_grad = gelu_back(pulled)[0].astype(jnp.bfloat16)
    grad_out = lax.dot_general(hidden, pin_grad, (((0,), (0,)), ((), ())), preferred_element_type=jnp.float32)
    grad_in = lax.dot_general(pin_feat, pre_grad, (((0,), (0,)), ((), ())), preferred_element_type=jnp.float32)
    grad_bias = lax.optimization_barrier(jnp.sum(pre_grad.astype(jnp.float32), axis=0))
    net_grad = lax.dot_general(onehot, pre_grad, (((0,), (0,)), ((), ())), preferred_element_type=jnp.float32).astype(jnp.bfloat16)
    grad_net = lax.dot_general(net_feat, net_grad, (((0,), (0,)), ((), ())), preferred_element_type=jnp.float32)
    feat_grad = (lax.dot_general(net_grad, w_net, (((1,), (1,)), ((), ())), preferred_element_type=jnp.float32) * inverse[:, None]).astype(jnp.bfloat16)
    pin_back = lax.dot_general(pre_grad, w_in, (((1,), (1,)), ((), ())), preferred_element_type=jnp.float32) + jnp.dot(onehot, feat_grad, preferred_element_type=jnp.float32)
    return (message, pin_back, (grad_in, grad_net, grad_bias, grad_out))

def reference(cell_feat, out_grad, w_in, w_net, bias, w_out, send_idx, pin_net, pin_ref, block_count):
    feat_dim = cell_feat.shape[1]
    hidden_dim = w_in.shape[1]
    grads_zero = (jnp.zeros((feat_dim, hidden_dim), jnp.float32), jnp.zeros((feat_dim, hidden_dim), jnp.float32), jnp.zeros((hidden_dim,), jnp.float32), jnp.zeros((hidden_dim, feat_dim), jnp.float32))
    initial = (jnp.zeros(cell_feat.shape, jnp.float32), jnp.zeros(cell_feat.shape, jnp.float32), grads_zero)

    def partition(part_no, running):
        acc_y, acc_x, gradients = running
        halo_rows = (jnp.arange(PARTITIONS, dtype=jnp.int32)[:, None] * CELL_DEV + send_idx[:, part_no, :].astype(jnp.int32)).reshape(-1).astype(jnp.int32)
        own_rows = (part_no * CELL_DEV + jnp.arange(CELL_DEV, dtype=jnp.int32)).astype(jnp.int32)
        table_rows = jnp.concatenate([own_rows, halo_rows])
        table_x = cell_feat[table_rows]
        table_g = out_grad[table_rows]
        local = (jnp.zeros((TABLE, feat_dim), jnp.float32), jnp.zeros((TABLE, feat_dim), jnp.float32), gradients)
        for net_no in range(NET_DEVS):

            def single_block(block_no, inner):
                local_y, local_x, grads_now = inner
                refs = pin_ref[part_no, net_no, block_no]
                message, pin_back, terms = block_pass(table_x, table_g, pin_net[part_no, net_no, block_no], refs, w_in, w_net, bias, w_out)
                return (local_y.at[refs].add(message), local_x.at[refs].add(pin_back), jax.tree.map(jnp.add, grads_now, terms))
            local = lax.fori_loop(0, block_count[part_no, net_no], single_block, local)
        return (acc_y.at[table_rows].add(local[0]), acc_x.at[table_rows].add(local[1]), local[2])
    acc_y, acc_x, gradients = lax.fori_loop(0, PARTITIONS, partition, initial)
    updated = (cell_feat.astype(jnp.float32) + acc_y).astype(jnp.bfloat16)
    cell_grad = (out_grad.astype(jnp.float32) + acc_x).astype(jnp.bfloat16)
    return (updated, cell_grad, gradients[0], gradients[1], gradients[2], gradients[3])
```

```python
import functools

import jax
import jax.numpy as jnp
from jax import lax
from jax.experimental import pallas as pl
from jax.experimental.pallas import tpu as pltpu
from jax.sharding import PartitionSpec as P

NETS_BLK = 128
BF16 = jnp.bfloat16
F32 = jnp.float32
VMEM_LIMIT = 48 * 1024 * 1024


def dot_nn(a, b):
    return jnp.dot(a, b, preferred_element_type=F32)


def dot_nt(a, b):
    return lax.dot_general(a, b, (((1,), (1,)), ((), ())), preferred_element_type=F32)


def dot_tn(a, b):
    return lax.dot_general(a, b, (((0,), (0,)), ((), ())), preferred_element_type=F32)


def slot_onehot(idx, cells):
    parts, slots = idx.shape
    lanes = parts * slots
    lane = lax.broadcasted_iota(jnp.int32, (slots, lanes), 1)
    spread = ((lane & (slots - 1)) == lax.broadcasted_iota(jnp.int32, (slots, lanes), 0)).astype(BF16)
    high = dot_nn((idx >> 6).astype(F32).astype(BF16), spread)
    low = dot_nn((idx & 63).astype(F32).astype(BF16), spread)
    wide = high * 64.0 + low
    lane = lax.broadcasted_iota(jnp.int32, (parts, lanes), 1)
    mine = (lane // slots) == lax.broadcasted_iota(jnp.int32, (parts, lanes), 0)
    row = jnp.sum(jnp.where(mine, wide, 0.0), axis=0, keepdims=True).astype(jnp.int32)
    return (lax.broadcasted_iota(jnp.int32, (cells, lanes), 0) == row).astype(BF16)


def gather_kernel(count_ref, idx_ref, x_ref, g_ref, net_ref, ref_ref, out_ref, ints_ref):
    part_count, slots = idx_ref.shape[1:]
    cells, feat = x_ref.shape
    group = 128 // slots
    for first in range(0, part_count, group):
        onehot = slot_onehot(idx_ref[0, first : first + group], cells)
        rows = pl.ds(first * slots, 128)
        out_ref[rows, :feat] = dot_tn(onehot, x_ref[...]).astype(BF16)
        out_ref[rows, feat:] = dot_tn(onehot, g_ref[...]).astype(BF16)
    slot_max = net_ref.shape[2]
    ints_ref[...] = jnp.full(ints_ref.shape, count_ref[0, 0], jnp.int32)
    ints_ref[:slot_max, :] = net_ref[0, 0]
    ints_ref[slot_max : 2 * slot_max, :] = ref_ref[0, 0]


def layer_kernel(
    split, pos_ref, x_ref, g_ref, halo_ref, ints_ref, w_in_ref, w_net_ref, bias_ref, w_out_ref, own_ref, *rest
):
    (*outs, table, win_t, wnet_t, wout_t, bias_t, nets, refs, acc, acc_in, acc_net, acc_out, acc_bias) = rest
    cells, feat = x_ref.shape
    hid = w_in_ref.shape[1]
    group_size, _, pins = ints_ref.shape
    part_count, slots = halo_ref.shape[:2]
    table_len = acc.shape[0]

    extra_net = jnp.zeros((1, pins), jnp.int32)
    extra_ref = jnp.zeros((1, pins), jnp.int32)
    for src in range(group_size):
        nets[src : src + 1, :] = ints_ref[src, 0:1, :]
        refs[src : src + 1, :] = ints_ref[src, 2:3, :]
        second = ints_ref[src, 4:5, :] > 1
        extra_net += jnp.where(second, ints_ref[src, 1:2, :] + 1, 0)
        extra_ref += jnp.where(second, ints_ref[src, 3:4, :] + 1, 0)
    nets[group_size : group_size + 1, :] = extra_net - 1
    refs[group_size : group_size + 1, :] = extra_ref - 1

    table[:feat, :cells] = x_ref[...].T
    table[feat:, :cells] = g_ref[...].T
    halo = halo_ref[...].reshape(part_count * slots, 2 * feat)
    table[:feat, cells:] = halo[:, :feat].T
    table[feat:, cells:] = halo[:, feat:].T
    win_t[...] = w_in_ref[...].T
    wnet_t[...] = w_net_ref[...].T
    wout_t[...] = w_out_ref[...].T
    bias_t[...] = jnp.broadcast_to(bias_ref[...], (128, hid)).T
    acc[...] = jnp.zeros_like(acc)
    acc_in[...] = jnp.zeros_like(acc_in)
    acc_net[...] = jnp.zeros_like(acc_net)
    acc_out[...] = jnp.zeros_like(acc_out)
    acc_bias[...] = jnp.zeros_like(acc_bias)
    ones = jnp.ones((8, pins), BF16)

    def block(b, carry):
        in_net = lax.broadcasted_iota(jnp.int32, (NETS_BLK, pins), 0) == nets[pl.ds(b, 1), :]
        in_net = in_net.astype(BF16)
        at_row = lax.broadcasted_iota(jnp.int32, (table_len, pins), 0) == refs[pl.ds(b, 1), :]
        at_row = at_row.astype(BF16)
        inverse = 1.0 / jnp.maximum(dot_nt(ones, in_net)[0:1], 1.0)
        taken = dot_nn(table[...], at_row).astype(BF16)
        feat_t, grad_t = taken[:feat], taken[feat:]
        net_feat = (dot_nt(feat_t, in_net) * inverse).astype(BF16)
        net_pre = dot_nn(wnet_t[...], net_feat).astype(BF16)
        bias_col = jnp.concatenate([bias_t[...]] * (pins // 128), axis=1)
        pre = dot_nn(win_t[...], feat_t) + dot_nn(net_pre, in_net) + bias_col
        pulled = dot_nn(w_out_ref[...], grad_t)
        square = pre * pre
        scale = 0.7978845608028654
        bend = jnp.tanh(pre * (scale + (scale * 0.044715) * square))
        half = 0.5 * bend + 0.5
        hidden = (pre * half).astype(BF16)
        slope = half + (0.5 * pre) * (1.0 - bend * bend) * (scale + (3 * scale * 0.044715) * square)
        pre_grad = (pulled * slope).astype(BF16)
        acc_out[...] += dot_nt(hidden, grad_t)
        acc_in[...] += dot_nt(feat_t, pre_grad)
        acc_bias[...] += dot_nt(ones, pre_grad)
        net_grad = dot_nt(pre_grad, in_net).astype(BF16)
        acc_net[...] += dot_nt(net_feat, net_grad)
        feat_grad = (dot_nn(w_net_ref[...], net_grad) * inverse).astype(BF16)
        message = dot_nn(wout_t[...], hidden).astype(BF16)
        back = (dot_nn(w_in_ref[...], pre_grad) + dot_nn(feat_grad, in_net)).astype(BF16)
        acc[...] += dot_nt(at_row, jnp.concatenate([message, back], axis=0))
        return carry

    lax.fori_loop(0, group_size + 1, block, 0)

    own_ref[...] = acc[:cells, :]
    if split:
        (send_ref,) = outs
        base = 3 * (feat // part_count)
    else:
        send_ref, grads_ref = outs
        base = 0
        grads_ref[:feat, :] = acc_in[...]
        grads_ref[feat : 2 * feat, :] = acc_net[...]
        grads_ref[2 * feat : 2 * feat + hid, :] = acc_out[...]
        grads_ref[2 * feat + hid :, :] = acc_bias[...]
    for part in range(part_count):
        if split:
            share = feat // part_count
            rows = slice(part * share, (part + 1) * share)
            send_ref[part, :share, :] = acc_in[rows, :].astype(BF16)
            send_ref[part, share : 2 * share, :] = acc_net[rows, :].astype(BF16)
            send_ref[part, 2 * share : 3 * share, :] = acc_out[rows, :].astype(BF16)
            bias_at = base + 2 * slots
            send_ref[part, bias_at : bias_at + 16, :] = jnp.broadcast_to(acc_bias[0:1, :], (16, hid)).astype(BF16)
        rows = slice(cells + part * slots, cells + (part + 1) * slots)
        send_ref[part, base : base + slots, :] = acc[rows, :feat].astype(BF16)
        send_ref[part, base + slots : base + 2 * slots, :] = acc[rows, feat:].astype(BF16)


def combine_kernel(split, pos_ref, idx_ref, got_ref, own_ref, *outs):
    part_count, slots = idx_ref.shape[1:]
    cells, wide = own_ref.shape
    feat = wide // 2
    base = 3 * (feat // part_count) if split else 0
    group = 128 // slots
    rows_y = own_ref[:, :feat]
    rows_x = own_ref[:, feat:]
    for first in range(0, part_count, group):
        onehot = slot_onehot(idx_ref[0, first : first + group], cells)
        y = got_ref[first : first + group, base : base + slots, :].reshape(128, feat)
        x = got_ref[first : first + group, base + slots : base + 2 * slots, :].reshape(128, feat)
        rows_y += dot_nn(onehot, y)
        rows_x += dot_nn(onehot, x)
    scratch = outs[-1]
    scratch[:, :feat] = rows_y
    scratch[:, feat:] = rows_x
    if split:
        piece_ref, *shares, _ = outs
        piece_ref[...] = jnp.sum(got_ref[:, :base, :].astype(F32), axis=0).astype(BF16)
        bias_at = base + 2 * slots
        bias = jnp.sum(got_ref[:, bias_at : bias_at + 16, :].astype(F32), axis=0)
    else:
        *shares, _ = outs
    group_size = len(shares)
    share = cells // group_size
    net = pos_ref[1]
    for k, share_ref in enumerate(shares):
        at = pl.multiple_of((net ^ k) * share, share)
        share_ref[:share, :] = scratch[pl.ds(at, share), :].astype(share_ref.dtype)
        if split:
            share_ref[share:, :feat] = bias.astype(share_ref.dtype)
            share_ref[share:, feat:] = jnp.zeros((16, feat), share_ref.dtype)


def rows_kernel(split, pos_ref, x_ref, g_ref, own_ref, *rest):
    updated_ref, back_ref = rest[-3:-1] if split else rest[-2:]
    others = rest[:-3] if split else rest[:-2]
    share, feat = x_ref.shape
    total = own_ref[:share, :]
    for other in others:
        total += other[:share, :].astype(F32)
    updated_ref[...] = (x_ref[...].astype(F32) + total[:, :feat]).astype(BF16)
    back_ref[...] = (g_ref[...].astype(F32) + total[:, feat:]).astype(BF16)
    if split:
        bias_ref = rest[-1]
        for k, part in enumerate((own_ref,) + tuple(others)):
            at = pl.multiple_of((pos_ref[1] ^ k) * feat, feat)
            bias_ref[:, pl.ds(at, feat)] = part[share : share + 1, :feat].astype(F32)


def place_kernel(tags, pos_ref, *refs):
    ins, (in_ref, net_ref, out_ref) = refs[:-3], refs[-3:]
    for ref, tag in zip(ins, tags):
        share = ref.shape[1] // 3
        hid = ref.shape[2]
        for at, (cell_bits, net_bits) in enumerate(tag):
            row = pl.multiple_of((pos_ref[0] ^ cell_bits) * share, share)
            first = pl.multiple_of((pos_ref[1] ^ net_bits) * hid, hid)
            in_ref[pl.ds(row, share), pl.ds(first, hid)] = ref[at, :share, :].astype(F32)
            net_ref[pl.ds(row, share), pl.ds(first, hid)] = ref[at, share : 2 * share, :].astype(F32)
            out_ref[pl.ds(pl.multiple_of(first + row, share), share), :] = ref[at, 2 * share :, :].astype(F32)


def whole(*shapes_and_specs):
    return [pl.BlockSpec(memory_space=pltpu.VMEM) for _ in range(shapes_and_specs[0])]


SMEM = pl.BlockSpec(memory_space=pltpu.SMEM)
PARAMS = dict(compiler_params=pltpu.CompilerParams(vmem_limit_bytes=VMEM_LIMIT))


def flip(x, axis, bits):
    size = lax.axis_size(axis)
    return lax.ppermute(x, axis, [(i, i ^ bits) for i in range(size)])


def gather_pieces(piece):
    near = [piece[None]] + [flip(piece, "cell", 2 * k)[None] for k in (1, 2, 3)]
    first = jnp.concatenate(near[:2])
    second = jnp.concatenate(near[2:])
    first = jnp.concatenate([first, flip(first, "cell", 1)])
    second = jnp.concatenate([second, flip(second, "net", 2)])
    first_tag = [(0, 0), (2, 0), (1, 0), (3, 0)]
    second_tag = [(4, 0), (6, 0), (4, 2), (6, 2)]
    all_of = jnp.concatenate([first, flip(first, "net", 2), second, flip(second, "cell", 1)])
    tag = (
        first_tag
        + [(a, b ^ 2) for a, b in first_tag]
        + second_tag
        + [(a ^ 1, b) for a, b in second_tag]
    )
    return [all_of, flip(all_of, "net", 1)], [tag, [(a, b ^ 1) for a, b in tag]]


def local(cell_feat, out_grad, w_in, w_net, bias, w_out, send_idx, pin_net, pin_ref, block_count):
    part_count = lax.axis_size("cell")
    group_size = lax.axis_size("net")
    cells, feat = cell_feat.shape
    hidden_dim = w_in.shape[1]
    hid = hidden_dim // group_size
    slots = send_idx.shape[2]
    pins = pin_net.shape[3]
    table_len = cells + part_count * slots
    split = part_count == 8 and group_size == 4
    pos = jnp.stack([lax.axis_index("cell"), lax.axis_index("net")]).astype(jnp.int32)

    sent, ints = pl.pallas_call(
        gather_kernel,
        in_specs=[SMEM] + whole(5),
        out_specs=whole(2),
        out_shape=[
            jax.ShapeDtypeStruct((part_count * slots, 2 * feat), BF16),
            jax.ShapeDtypeStruct((8, pins), jnp.int32),
        ],
        name="take_boundary",
        **PARAMS,
    )(block_count, send_idx, cell_feat, out_grad, pin_net, pin_ref)
    halo = lax.all_to_all(
        sent.reshape(part_count, slots, 2 * feat), "cell", split_axis=0, concat_axis=0, tiled=True
    )
    all_ints = lax.all_gather(ints, "net")

    base = 3 * (feat // part_count) if split else 0
    send_rows = base + 2 * slots + (16 if split else 0)
    out_shape = [
        jax.ShapeDtypeStruct((cells, 2 * feat), F32),
        jax.ShapeDtypeStruct((part_count, send_rows, feat), BF16),
    ]
    if not split:
        out_shape.append(jax.ShapeDtypeStruct((2 * feat + hid + 8, hid), F32))

    def full(*shape):
        return pl.BlockSpec(shape, lambda i, pos: (0,) * len(shape))

    own, send, *grads = pl.pallas_call(
        functools.partial(layer_kernel, split),
        grid_spec=pltpu.PrefetchScalarGridSpec(
            num_scalar_prefetch=1,
            grid=(1,),
            in_specs=[
                full(cells, feat),
                full(cells, feat),
                full(part_count, slots, 2 * feat),
                full(group_size, 8, pins),
                pl.BlockSpec((feat, hid), lambda i, pos: (0, pos[1])),
                pl.BlockSpec((feat, hid), lambda i, pos: (0, pos[1])),
                pl.BlockSpec((1, hid), lambda i, pos: (0, pos[1])),
                pl.BlockSpec((hid, feat), lambda i, pos: (pos[1], 0)),
            ],
            out_specs=[full(*s.shape) for s in out_shape],
            scratch_shapes=[
                pltpu.VMEM((2 * feat, table_len), BF16),
                pltpu.VMEM((hid, feat), BF16),
                pltpu.VMEM((hid, feat), BF16),
                pltpu.VMEM((feat, hid), BF16),
                pltpu.VMEM((hid, 128), F32),
                pltpu.VMEM((8 * (-(-(group_size + 1) // 8)), pins), jnp.int32),
                pltpu.VMEM((8 * (-(-(group_size + 1) // 8)), pins), jnp.int32),
                pltpu.VMEM((table_len, 2 * feat), F32),
                pltpu.VMEM((feat, hid), F32),
                pltpu.VMEM((feat, hid), F32),
                pltpu.VMEM((hid, feat), F32),
                pltpu.VMEM((8, hid), F32),
            ],
        ),
        out_shape=out_shape,
        name="layer",
        **PARAMS,
    )(pos, cell_feat, out_grad, halo, all_ints, w_in, w_net, bias.reshape(1, hidden_dim), w_out)

    got = lax.all_to_all(send, "cell", split_axis=0, concat_axis=0, tiled=True)
    share = cells // group_size
    share_rows = share + (16 if split else 0)
    out_shape = [jax.ShapeDtypeStruct((share_rows, 2 * feat), F32 if k == 0 else BF16) for k in range(group_size)]
    if split:
        out_shape = [jax.ShapeDtypeStruct((base, feat), BF16)] + out_shape
    outs = pl.pallas_call(
        functools.partial(combine_kernel, split),
        in_specs=[SMEM] + whole(3),
        out_specs=whole(len(out_shape)),
        out_shape=out_shape,
        scratch_shapes=[pltpu.VMEM((cells, 2 * feat), F32)],
        name="combine",
        **PARAMS,
    )(pos, send_idx, got, own)
    shares = outs[1:] if split else outs
    received = [flip(shares[k], "net", k) for k in range(1, group_size)]

    def mine(i, pos):
        return (pos[1], 0)

    out_shape = [jax.ShapeDtypeStruct((share, feat), BF16)] * 2
    if split:
        out_shape.append(jax.ShapeDtypeStruct((1, hidden_dim), F32))
    rows = pl.pallas_call(
        functools.partial(rows_kernel, split),
        grid_spec=pltpu.PrefetchScalarGridSpec(
            num_scalar_prefetch=1,
            grid=(1,),
            in_specs=[pl.BlockSpec((share, feat), mine)] * 2 + [full(share_rows, 2 * feat)] * group_size,
            out_specs=[full(*s.shape) for s in out_shape],
        ),
        out_shape=out_shape,
        name="own_rows",
        **PARAMS,
    )(pos, cell_feat, out_grad, shares[0], *received)
    if split:
        pieces, tags = gather_pieces(outs[0])
        grad_in, grad_net, grad_out = pl.pallas_call(
            functools.partial(place_kernel, tags),
            in_specs=[SMEM] + whole(len(pieces)),
            out_specs=whole(3),
            out_shape=[
                jax.ShapeDtypeStruct((feat, hidden_dim), F32),
                jax.ShapeDtypeStruct((feat, hidden_dim), F32),
                jax.ShapeDtypeStruct((hidden_dim, feat), F32),
            ],
            name="place",
            **PARAMS,
        )(pos, *pieces)
        return (rows[0], rows[1], grad_in, grad_net, rows[2].reshape(hidden_dim), grad_out)
    summed = lax.all_gather(lax.psum(grads[0], "cell"), "net")
    grad_in = jnp.moveaxis(summed[:, :feat], 0, 1).reshape(feat, hidden_dim)
    grad_net = jnp.moveaxis(summed[:, feat : 2 * feat], 0, 1).reshape(feat, hidden_dim)
    grad_out = summed[:, 2 * feat : 2 * feat + hid].reshape(hidden_dim, feat)
    grad_bias = summed[:, 2 * feat + hid].reshape(hidden_dim)
    return (rows[0], rows[1], grad_in, grad_net, grad_bias, grad_out)


def solution(mesh):
    placed = (
        P("cell", None),
        P("cell", None),
        P(),
        P(),
        P(),
        P(),
        P("cell", None, None),
        P("cell", "net", None, None),
        P("cell", "net", None, None),
        P("cell", "net"),
    )
    return jax.shard_map(
        local,
        mesh=mesh,
        in_specs=placed,
        out_specs=(P(("cell", "net"), None), P(("cell", "net"), None), P(), P(), P(), P()),
        check_vma=False,
    )
```

```python
import functools

import jax
import jax.numpy as jnp
from jax import lax
from jax.experimental import pallas as pl
from jax.experimental.pallas import tpu as pltpu
from jax.sharding import PartitionSpec as P

NETS_BLK = 128
BF16 = jnp.bfloat16
F32 = jnp.float32
VMEM_LIMIT = 40 * 1024 * 1024


def dot_nn(a, b):
    return jnp.dot(a, b, preferred_element_type=F32)


def dot_nt(a, b):
    return lax.dot_general(a, b, (((1,), (1,)), ((), ())), preferred_element_type=F32)


def dot_tn(a, b):
    return lax.dot_general(a, b, (((0,), (0,)), ((), ())), preferred_element_type=F32)


def slot_onehot(idx, first, cells):
    parts, slots = idx.shape
    lanes = parts * slots
    lane = lax.broadcasted_iota(jnp.int32, (slots, lanes), 1)
    spread = ((lane & (slots - 1)) == lax.broadcasted_iota(jnp.int32, (slots, lanes), 0)).astype(BF16)
    high = dot_nn((idx >> 6).astype(F32).astype(BF16), spread)
    low = dot_nn((idx & 63).astype(F32).astype(BF16), spread)
    wide = high * 64.0 + low
    lane = lax.broadcasted_iota(jnp.int32, (parts, lanes), 1)
    mine = (lane // slots) == lax.broadcasted_iota(jnp.int32, (parts, lanes), 0)
    row = jnp.sum(jnp.where(mine, wide, 0.0), axis=0, keepdims=True).astype(jnp.int32) - first
    return (lax.broadcasted_iota(jnp.int32, (cells, lanes), 0) == row).astype(BF16)


def idx_rows(idx_ref, parts):
    return jnp.concatenate([idx_ref[0, pl.ds(part, 1), :] for part in parts], axis=0)


def start_copies(pairs, sems):
    copies = [pltpu.make_async_copy(src, dst, sems.at[i]) for i, (src, dst) in enumerate(pairs)]
    for copy in copies:
        copy.start()
    return copies


def gather_kernel(count_ref, idx_hbm, x_hbm, g_hbm, net_hbm, ref_hbm, out_ref, ints_ref, *scratch):
    idx_ref, x_ref, g_ref, net_ref, ref_ref, sems = scratch
    copies = start_copies(
        [(idx_hbm, idx_ref), (x_hbm, x_ref), (g_hbm, g_ref), (net_hbm, net_ref), (ref_hbm, ref_ref)], sems
    )
    for copy in copies:
        copy.wait()
    part_count, slots = idx_ref.shape[1:]
    cells, feat = x_ref.shape
    group = 128 // slots
    for first in range(0, part_count, group):
        onehot = slot_onehot(idx_ref[0, first : first + group], 0, cells)
        for at, values in ((0, x_ref), (feat, g_ref)):
            rows = dot_tn(onehot, values[...]).astype(BF16)
            out_ref[first : first + group, :, at : at + feat] = rows.reshape(group, slots, feat)
    slot_max = net_ref.shape[2]
    ints_ref[0] = jnp.broadcast_to(count_ref[...], ints_ref.shape[1:])
    ints_ref[0, :slot_max, :] = net_ref[0, 0]
    ints_ref[0, slot_max : 2 * slot_max, :] = ref_ref[0, 0]


def split_bf16(x):
    high = x.astype(BF16)
    return high, (x - high.astype(F32)).astype(BF16)


def block_ids(ints_refs):
    nets, refs = [], []
    pins = ints_refs[0].shape[2]
    extra_net = jnp.zeros((1, pins), jnp.int32)
    extra_ref = jnp.zeros((1, pins), jnp.int32)
    for ints in [ref[i] for ref in ints_refs for i in range(ref.shape[0])]:
        nets.append(ints[0:1, :])
        refs.append(ints[2:3, :])
        second = ints[4:5, :] > 1
        extra_net += jnp.where(second, ints[1:2, :] + 1, 0)
        extra_ref += jnp.where(second, ints[3:4, :] + 1, 0)
    nets.append(extra_net - 1)
    refs.append(extra_ref - 1)
    return nets, refs


def row_onehot(rows, ids):
    return (lax.broadcasted_iota(jnp.int32, (rows, ids.shape[1]), 0) == ids).astype(BF16)


def column_onehot(ids, lanes):
    return (lax.broadcasted_iota(jnp.int32, (ids.shape[0], lanes), 1) == ids).astype(BF16)


def net_inverse(pin_net):
    return 1.0 / jnp.maximum(jnp.sum(pin_net.astype(F32), axis=1, keepdims=True), 1.0)


def layer_kernel(fast, pos_ref, halo_ref, *rest):
    ints_refs, rest = rest[:-26], rest[-26:]
    x_hbm, g_hbm, w_in_hbm, w_net_hbm, bias_hbm, w_out_hbm, grads_ref, ids_hbm, sums_hbm, net_grads_hbm, *rest = rest
    table, w_in_ref, w_net_ref, bias_ref, w_out_ref, in_sems, ids, sums, net_grads, out_sems, *rest = rest
    at_pin, at_row, net_pin, taken, net_feats, terms = rest
    cells, feat = x_hbm.shape
    hid = w_in_ref.shape[1]
    pin_count, table_len = at_pin.shape
    blocks = net_grads.shape[0] // NETS_BLK
    pins = pin_count // blocks
    mine = pl.ds(pl.multiple_of(pos_ref[1] * hid, hid), hid)
    copies = start_copies(
        [
            (x_hbm, table.at[:cells, :feat]),
            (g_hbm, table.at[:cells, feat:]),
            (w_net_hbm.at[:, mine], w_net_ref),
            (w_in_hbm.at[:, mine], w_in_ref),
            (bias_hbm.at[:, mine], bias_ref),
            (w_out_hbm.at[mine, :], w_out_ref),
        ],
        in_sems,
    )
    table[cells:, :] = halo_ref[...].reshape(table_len - cells, 2 * feat)
    nets, refs = block_ids(ints_refs)
    ids[...] = jnp.zeros_like(ids)
    for b in range(blocks):
        ids[b : b + 1, :] = nets[b].astype(F32)
        ids[64 + b : 65 + b, :] = refs[b].astype(F32)
    columns = ids[...].T.astype(jnp.int32)
    for b in range(blocks):
        of = slice(b * pins, (b + 1) * pins)
        at_pin[of, :] = column_onehot(columns[:, 64 + b : 65 + b], table_len)
        net_pin[of, :] = column_onehot(columns[:, b : b + 1], NETS_BLK)
        at_row[:, of] = row_onehot(table_len, refs[b])
    pin_nets = [row_onehot(NETS_BLK, net) for net in nets]
    for copy in copies:
        copy.wait()
    outgoing = start_copies([(ids, ids_hbm)], out_sems)
    for b in range(blocks):
        of = slice(b * pins, (b + 1) * pins)
        nets_of = slice(b * NETS_BLK, (b + 1) * NETS_BLK)
        taken[of, :] = dot_nn(at_pin[of, :], table[...]).astype(BF16)
        net_sum = dot_nn(pin_nets[b], taken[of, :feat])
        net_feats[nets_of, :] = (net_sum * net_inverse(pin_nets[b])).astype(BF16)
    net_pre = dot_nn(net_feats[...], w_net_ref[...]).astype(BF16)
    scale = 0.7978845608028654
    for b in range(blocks):
        of = slice(b * pins, (b + 1) * pins)
        nets_of = slice(b * NETS_BLK, (b + 1) * NETS_BLK)
        pre = dot_nn(taken[of, :feat], w_in_ref[...]) + dot_nn(net_pin[of, :], net_pre[nets_of]) + bias_ref[...]
        pulled = dot_nt(taken[of, feat:], w_out_ref[...])
        square = pre * pre
        bend = jnp.tanh(pre * (scale + (scale * 0.044715) * square))
        half = 0.5 * bend + 0.5
        terms[of, :hid] = (pre * half).astype(BF16)
        slope = half + (0.5 * pre) * (1.0 - bend * bend) * (scale + (3 * scale * 0.044715) * square)
        pre_grad = (pulled * slope).astype(BF16)
        terms[of, hid:] = pre_grad
        net_grads[nets_of, :] = dot_nn(pin_nets[b], pre_grad).astype(BF16)
    sums[...] = dot_nn(at_row[...], terms[...])
    outgoing += start_copies([(sums, sums_hbm), (net_grads, net_grads_hbm)], out_sems.at[1:])
    hidden_high, hidden_low = split_bf16(sums[:, :hid])
    grad_high, grad_low = split_bf16(sums[:, hid:])
    table_x, table_g = table[:, :feat], table[:, feat:]
    acc_in = dot_tn(table_x, grad_high) + dot_tn(table_x, grad_low)
    acc_out = dot_tn(hidden_high, table_g) + dot_tn(hidden_low, table_g)
    acc_net = dot_tn(net_feats[...], net_grads[...])
    acc_bias = jnp.broadcast_to(jnp.sum(sums[:, hid:], axis=0, keepdims=True), (8, hid))
    if fast:
        part_count, rows, _ = grads_ref.shape
        part = feat // part_count
        for to in range(part_count):
            of = slice(to * part, (to + 1) * part)
            blocks_of = [acc_in[of, :], acc_net[of, :], acc_out[of, :], acc_bias]
            grads_ref[to] = jnp.concatenate([x.astype(BF16) for x in blocks_of], axis=0)
    else:
        grads_ref[:feat, :] = acc_in
        grads_ref[feat : 2 * feat, :] = acc_net
        grads_ref[2 * feat : 2 * feat + hid, :] = acc_out
        grads_ref[2 * feat + hid :, :] = acc_bias
    for copy in outgoing:
        copy.wait()


def back_kernel(fast, pos_ref, ids_hbm, sums_hbm, net_grads_hbm, w_in_hbm, w_net_hbm, w_out_hbm, *rest):
    *outs, ids, sums, net_grads, w_in_ref, w_net_ref, w_out_ref, sems, at_row, net_backs, acc = rest
    table_len, wide = acc.shape
    feat, hid = w_in_ref.shape
    blocks = net_grads.shape[0] // NETS_BLK
    pins = ids.shape[1]
    mine = pl.ds(pl.multiple_of(pos_ref[1] * hid, hid), hid)
    copies = start_copies(
        [
            (ids_hbm, ids),
            (net_grads_hbm, net_grads),
            (w_net_hbm.at[:, mine], w_net_ref),
            (w_in_hbm.at[:, mine], w_in_ref),
            (w_out_hbm.at[mine, :], w_out_ref),
            (sums_hbm, sums),
        ],
        sems,
    )
    for copy in copies:
        copy.wait()
    columns = ids[...].T.astype(jnp.int32)
    rows = ids[...].astype(jnp.int32)
    for b in range(blocks):
        of = slice(b * pins, (b + 1) * pins)
        nets_of = slice(b * NETS_BLK, (b + 1) * NETS_BLK)
        at_row[:, of] = row_onehot(table_len, rows[64 + b : 65 + b, :])
        inverse = net_inverse(row_onehot(NETS_BLK, rows[b : b + 1, :]))
        feat_grad = (dot_nt(net_grads[nets_of, :], w_net_ref[...]) * inverse).astype(BF16)
        net_backs[of, :] = dot_nn(column_onehot(columns[:, b : b + 1], NETS_BLK), feat_grad).astype(BF16)
    hidden_high, hidden_low = split_bf16(sums[:, :hid])
    grad_high, grad_low = split_bf16(sums[:, hid:])
    acc[:, :feat] = dot_nn(hidden_high, w_out_ref[...]) + dot_nn(hidden_low, w_out_ref[...])
    acc[:, feat:] = (
        dot_nt(grad_high, w_in_ref[...]) + dot_nt(grad_low, w_in_ref[...]) + dot_nn(at_row[...], net_backs[...])
    )
    if fast:
        group_size = len(outs)
        share = (table_len - 128) // group_size
        cells = share * group_size
        for bits, share_ref in enumerate(outs):
            to = pos_ref[1] ^ bits
            rows = acc[pl.ds(pl.multiple_of(to * share, share), share), :]
            share_ref[:share, :] = rows.astype(share_ref.dtype)
            for odd in range(2):
                part = pos_ref[0] ^ (2 * to + odd)
                edge = acc[pl.ds(pl.multiple_of(cells + part * 16, 16), 16), :]
                share_ref[share + 16 * odd : share + 16 * (odd + 1), :] = edge.astype(share_ref.dtype)
        return
    own_ref, send_ref = outs
    cells = own_ref.shape[0]
    own_ref[...] = acc[:cells, :]
    part_count, rows, _ = send_ref.shape
    slots = rows // 2
    for part in range(part_count):
        of = slice(cells + part * slots, cells + (part + 1) * slots)
        send_ref[part, :slots, :] = acc[of, :feat].astype(BF16)
        send_ref[part, slots:, :] = acc[of, feat:].astype(BF16)


def sum_shares_kernel(after_ref, own_ref, *rest):
    *others, rows_ref, even_ref, odd_ref = rest
    total = own_ref[...]
    for other in others:
        total += other[...].astype(F32)
    share = rows_ref.shape[0]
    slots = even_ref.shape[0]
    rows_ref[...] = total[:share]
    even_ref[...] = total[share : share + slots].astype(BF16)
    odd_ref[...] = total[share + slots :].astype(BF16)


def sum_pieces_kernel(got_ref, piece_ref, bias_ref):
    total = got_ref[0].astype(F32)
    for part in range(1, got_ref.shape[0]):
        total += got_ref[part].astype(F32)
    rows = piece_ref.shape[0]
    piece_ref[...] = total[:rows].astype(BF16)
    bias_ref[...] = jnp.concatenate([jnp.concatenate([total[rows:]] * 2, axis=0)] * 2, axis=1).astype(BF16)


def rows_kernel(pos_ref, idx_ref, x_hbm, g_hbm, rows_ref, *rest):
    *edges, updated_ref, back_ref, bias_ref, x_ref, g_ref, sems = rest
    share, feat = updated_ref.shape
    net = pos_ref[1]
    mine = pl.ds(pl.multiple_of(net * share, share), share)
    copies = start_copies([(x_hbm.at[mine, :], x_ref), (g_hbm.at[mine, :], g_ref)], sems)
    order = [pos_ref[0] ^ (2 * (net ^ bits) + odd) for bits in range(len(edges)) for odd in range(2)]
    onehot = slot_onehot(idx_rows(idx_ref, order), net * share, share)
    halo = jnp.concatenate([edge[:32, :] for edge in edges], axis=0)
    total = rows_ref[...] + dot_nn(onehot, halo)
    for bits, edge in enumerate(edges):
        at = pl.multiple_of((net ^ bits) * feat, feat)
        bias_ref[:, pl.ds(at, feat)] = edge[32:, :feat].astype(F32)[:1]
    for copy in copies:
        copy.wait()
    updated_ref[...] = (x_ref[...].astype(F32) + total[:, :feat]).astype(BF16)
    back_ref[...] = (g_ref[...].astype(F32) + total[:, feat:]).astype(BF16)


def place_kernel(tags, olds, pos_ref, *refs):
    ins, refs = refs[: len(tags)], refs[len(tags) + olds :]
    outs, (buffer, sems) = refs[:3], refs[3:]
    part = ins[0].shape[1] // 3
    hid = ins[0].shape[2]
    columns = sorted({net_bits for tag in tags for _, net_bits in tag})
    copies = []
    for matrix in range(3):
        for column, net_bits in enumerate(columns):
            at = matrix * len(columns) + column
            for ref, tag in zip(ins, tags):
                for piece, (cell_bits, bits) in enumerate(tag):
                    if bits == net_bits:
                        row = pl.multiple_of((pos_ref[0] ^ cell_bits) * part, part)
                        values = ref[piece, matrix * part : (matrix + 1) * part, :].astype(F32)
                        buffer[at, pl.ds(row, part), :] = values
            first = pl.ds(pl.multiple_of((pos_ref[1] ^ net_bits) * hid, hid), hid)
            target = outs[2].at[first, :] if matrix == 2 else outs[matrix].at[:, first]
            copy = pltpu.make_async_copy(buffer.at[at], target, sems.at[at])
            copy.start()
            copies.append(copy)
    for copy in copies:
        copy.wait()


def combine_kernel(pos_ref, idx_ref, got_ref, own_ref, *outs):
    part_count, slots = idx_ref.shape[1:]
    cells, wide = own_ref.shape
    feat = wide // 2
    group = 128 // slots
    rows_y = own_ref[:, :feat]
    rows_x = own_ref[:, feat:]
    for first in range(0, part_count, group):
        onehot = slot_onehot(idx_ref[0, first : first + group], 0, cells)
        y = got_ref[first : first + group, :slots, :].reshape(128, feat)
        x = got_ref[first : first + group, slots:, :].reshape(128, feat)
        rows_y += dot_nn(onehot, y)
        rows_x += dot_nn(onehot, x)
    *shares, scratch = outs
    scratch[:, :feat] = rows_y
    scratch[:, feat:] = rows_x
    share = cells // len(shares)
    for bits, share_ref in enumerate(shares):
        at = pl.multiple_of((pos_ref[1] ^ bits) * share, share)
        share_ref[...] = scratch[pl.ds(at, share), :].astype(share_ref.dtype)


def plain_rows_kernel(pos_ref, x_hbm, g_hbm, own_ref, *rest):
    *others, updated_ref, back_ref, x_ref, g_ref, sems = rest
    share, feat = updated_ref.shape
    mine = pl.ds(pl.multiple_of(pos_ref[1] * share, share), share)
    copies = start_copies([(x_hbm.at[mine, :], x_ref), (g_hbm.at[mine, :], g_ref)], sems)
    total = own_ref[...]
    for other in others:
        total += other[...].astype(F32)
    for copy in copies:
        copy.wait()
    updated_ref[...] = (x_ref[...].astype(F32) + total[:, :feat]).astype(BF16)
    back_ref[...] = (g_ref[...].astype(F32) + total[:, feat:]).astype(BF16)


def whole(count):
    return [pl.BlockSpec(memory_space=pltpu.VMEM)] * count


SMEM = pl.BlockSpec(memory_space=pltpu.SMEM)
HBM = pl.BlockSpec(memory_space=pltpu.HBM)
PARAMS = dict(compiler_params=pltpu.CompilerParams(vmem_limit_bytes=VMEM_LIMIT))


def in_hbm(*arrays):
    return [pltpu.with_memory_space_constraint(x, pltpu.HBM) for x in arrays]


def flip(x, axis, bits):
    size = lax.axis_size(axis)
    return lax.ppermute(x, axis, [(i, i ^ bits) for i in range(size)])


def both(x, cell_bits, net_bits):
    parts, group = lax.axis_size("cell"), lax.axis_size("net")
    pairs = [
        (c * group + n, (c ^ cell_bits(n)) * group + (n ^ net_bits)) for c in range(parts) for n in range(group)
    ]
    return lax.ppermute(x, ("cell", "net"), pairs)


def local(cell_feat, out_grad, w_in, w_net, bias, w_out, send_idx, pin_net, pin_ref, block_count):
    part_count = lax.axis_size("cell")
    group_size = lax.axis_size("net")
    cells, feat = cell_feat.shape
    hidden_dim = w_in.shape[1]
    hid = hidden_dim // group_size
    slots = send_idx.shape[2]
    pins = pin_net.shape[3]
    table_len = cells + part_count * slots
    fast = part_count == 8 and group_size == 4
    pos = jnp.stack([lax.axis_index("cell"), lax.axis_index("net")]).astype(jnp.int32)

    def shape(dtype, *dims):
        return jax.ShapeDtypeStruct(dims, dtype)

    sent, ints = pl.pallas_call(
        gather_kernel,
        in_specs=whole(1) + [HBM] * 5,
        out_specs=whole(2),
        out_shape=[shape(BF16, part_count, slots, 2 * feat), shape(jnp.int32, 1, 8, pins)],
        scratch_shapes=[
            pltpu.VMEM(send_idx.shape, jnp.int32),
            pltpu.VMEM((cells, feat), BF16),
            pltpu.VMEM((cells, feat), BF16),
            pltpu.VMEM(pin_net.shape, jnp.int32),
            pltpu.VMEM(pin_ref.shape, jnp.int32),
            pltpu.SemaphoreType.DMA((5,)),
        ],
        name="take_boundary",
        **PARAMS,
    )(block_count, *in_hbm(send_idx, cell_feat, out_grad, pin_net, pin_ref))
    halo = lax.all_to_all(sent, "cell", split_axis=0, concat_axis=0, tiled=True)
    if fast:
        all_ints = [ints] + [flip(ints, "net", bits) for bits in range(1, group_size)]
    else:
        all_ints = [lax.all_gather(ints, "net", tiled=True)]

    blocks = group_size + 1
    part = feat // part_count
    share = cells // group_size
    edge = part_count * slots // group_size
    weights = [w_in, w_net, bias.reshape(1, hidden_dim), w_out]
    grads, ids, sums, net_grads = pl.pallas_call(
        functools.partial(layer_kernel, fast),
        in_specs=[SMEM] + whole(1 + len(all_ints)) + [HBM] * 6,
        out_specs=whole(1) + [HBM] * 3,
        out_shape=[
            shape(BF16, part_count, 3 * part + 8, feat) if fast else shape(F32, 2 * feat + hid + 8, hid),
            pltpu.HBM((128, pins), F32),
            pltpu.HBM((table_len, 2 * hid), F32),
            pltpu.HBM((blocks * NETS_BLK, hid), BF16),
        ],
        scratch_shapes=[
            pltpu.VMEM((table_len, 2 * feat), BF16),
            pltpu.VMEM((feat, hid), BF16),
            pltpu.VMEM((feat, hid), BF16),
            pltpu.VMEM((1, hid), F32),
            pltpu.VMEM((hid, feat), BF16),
            pltpu.SemaphoreType.DMA((6,)),
            pltpu.VMEM((128, pins), F32),
            pltpu.VMEM((table_len, 2 * hid), F32),
            pltpu.VMEM((blocks * NETS_BLK, hid), BF16),
            pltpu.SemaphoreType.DMA((3,)),
            pltpu.VMEM((blocks * pins, table_len), BF16),
            pltpu.VMEM((table_len, blocks * pins), BF16),
            pltpu.VMEM((blocks * pins, NETS_BLK), BF16),
            pltpu.VMEM((blocks * pins, 2 * feat), BF16),
            pltpu.VMEM((blocks * NETS_BLK, feat), BF16),
            pltpu.VMEM((blocks * pins, 2 * hid), BF16),
        ],
        name="layer",
        **PARAMS,
    )(pos, halo, *all_ints, *in_hbm(cell_feat, out_grad, *weights))

    if fast:
        got = lax.all_to_all(grads, "cell", split_axis=0, concat_axis=0, tiled=True)
        out_shape = [shape(BF16 if bits else F32, share + edge, 2 * feat) for bits in range(group_size)]
    else:
        out_shape = [shape(F32, cells, 2 * feat), shape(BF16, part_count, 2 * slots, feat)]
    outs = pl.pallas_call(
        functools.partial(back_kernel, fast),
        in_specs=[SMEM] + [HBM] * 6,
        out_specs=whole(len(out_shape)),
        out_shape=out_shape,
        scratch_shapes=[
            pltpu.VMEM((128, pins), F32),
            pltpu.VMEM((table_len, 2 * hid), F32),
            pltpu.VMEM((blocks * NETS_BLK, hid), BF16),
            pltpu.VMEM((feat, hid), BF16),
            pltpu.VMEM((feat, hid), BF16),
            pltpu.VMEM((hid, feat), BF16),
            pltpu.SemaphoreType.DMA((6,)),
            pltpu.VMEM((table_len, blocks * pins), BF16),
            pltpu.VMEM((blocks * pins, feat), BF16),
            pltpu.VMEM((table_len, 2 * feat), F32),
        ],
        name="back",
        **PARAMS,
    )(pos, *in_hbm(ids, sums, net_grads, w_in, w_net, w_out))

    row_shapes = [shape(BF16, share, feat)] * 2
    row_scratch = [
        pltpu.VMEM((share, feat), BF16),
        pltpu.VMEM((share, feat), BF16),
        pltpu.SemaphoreType.DMA((2,)),
    ]
    grad_shapes = [shape(F32, feat, hidden_dim), shape(F32, feat, hidden_dim), shape(F32, hidden_dim, feat)]
    if not fast:
        own, send = outs
        got = lax.all_to_all(send, "cell", split_axis=0, concat_axis=0, tiled=True)
        shares = pl.pallas_call(
            combine_kernel,
            in_specs=[SMEM] + whole(3),
            out_specs=whole(group_size),
            out_shape=[shape(BF16 if bits else F32, share, 2 * feat) for bits in range(group_size)],
            scratch_shapes=[pltpu.VMEM((cells, 2 * feat), F32)],
            name="combine",
            **PARAMS,
        )(pos, send_idx, got, own)
        others = [flip(shares[bits], "net", bits) for bits in range(1, group_size)]
        updated, cell_grad = pl.pallas_call(
            plain_rows_kernel,
            in_specs=[SMEM] + [HBM] * 2 + whole(group_size),
            out_specs=whole(2),
            out_shape=row_shapes,
            scratch_shapes=row_scratch,
            name="own_rows",
            **PARAMS,
        )(pos, *in_hbm(cell_feat, out_grad), shares[0], *others)
        summed = lax.all_gather(lax.psum(grads, "cell"), "net")
        grad_in = jnp.moveaxis(summed[:, :feat], 0, 1).reshape(feat, hidden_dim)
        grad_net = jnp.moveaxis(summed[:, feat : 2 * feat], 0, 1).reshape(feat, hidden_dim)
        grad_out = summed[:, 2 * feat : 2 * feat + hid].reshape(hidden_dim, feat)
        grad_bias = summed[:, 2 * feat + hid].reshape(hidden_dim)
        return (updated, cell_grad, grad_in, grad_net, grad_bias, grad_out)

    shares = outs
    others = [flip(shares[bits], "net", bits) for bits in range(1, group_size)]
    piece, bias_sum = pl.pallas_call(
        sum_pieces_kernel,
        in_specs=whole(1),
        out_specs=whole(2),
        out_shape=[shape(BF16, 3 * part, feat), shape(BF16, 16, 2 * feat)],
        name="sum_pieces",
        **PARAMS,
    )(got)
    rows, even, odd = pl.pallas_call(
        sum_shares_kernel,
        in_specs=[pl.BlockSpec(memory_space=pl.ANY)] + whole(group_size),
        out_specs=whole(3),
        out_shape=[shape(F32, share, 2 * feat), shape(BF16, slots, 2 * feat), shape(BF16, slots, 2 * feat)],
        name="sum_shares",
        **PARAMS,
    )(piece, shares[0], *others)
    near = [flip(piece, "cell", 2 * k) for k in (1, 2, 3)]
    even = both(even, lambda n: 2 * n, 0)
    odd = both(odd, lambda n: 2 * n + 1, 0)
    near, even, odd = lax.optimization_barrier((near, even, odd))
    edges = jnp.concatenate([even, odd, bias_sum])
    other_edges = [flip(edges, "net", bits) for bits in range(1, group_size)]
    first, second = jnp.stack([piece, near[0]]), jnp.stack(near[1:])
    first = jnp.concatenate([first, flip(first, "cell", 1)])
    second = jnp.concatenate([second, flip(second, "net", 2)])
    early = [flip(first, "net", 1), flip(second, "net", 1)]
    third, fourth = flip(first, "net", 2), flip(second, "cell", 1)
    first_tag = [(0, 0), (2, 0), (1, 0), (3, 0)]
    second_tag = [(4, 0), (6, 0), (4, 2), (6, 2)]
    tags = [first_tag, second_tag, [(a, b ^ 2) for a, b in first_tag], [(a ^ 1, b) for a, b in second_tag]]
    twin_tags = [[(a, b ^ 1) for a, b in tag] for tag in tags]

    updated, cell_grad, grad_bias = pl.pallas_call(
        rows_kernel,
        in_specs=[SMEM] + whole(1) + [HBM] * 2 + whole(1 + group_size),
        out_specs=whole(3),
        out_shape=row_shapes + [shape(F32, 1, hidden_dim)],
        scratch_shapes=row_scratch,
        name="own_rows",
        **PARAMS,
    )(pos, send_idx, *in_hbm(cell_feat, out_grad), rows, edges, *other_edges)

    third, fourth, updated, cell_grad = lax.optimization_barrier((third, fourth, updated, cell_grad))
    late = [flip(third, "net", 1), flip(fourth, "net", 1)]

    def place(arrays, tags, olds):
        return pl.pallas_call(
            functools.partial(place_kernel, tags, len(olds)),
            in_specs=[SMEM] + whole(len(arrays)) + [HBM] * len(olds),
            out_specs=[HBM] * 3,
            out_shape=grad_shapes,
            scratch_shapes=[pltpu.VMEM((6, feat, hid), F32), pltpu.SemaphoreType.DMA((6,))],
            input_output_aliases={1 + len(arrays) + i: i for i in range(len(olds))},
            name="place",
            **PARAMS,
        )(pos, *arrays, *olds)

    grads = place([first, second, third, fourth], tags, [])
    grad_in, grad_net, grad_out = place(early + late, twin_tags, grads)
    return (updated, cell_grad, grad_in, grad_net, grad_bias.reshape(hidden_dim), grad_out)


def solution(mesh):
    placed = (
        P("cell", None),
        P("cell", None),
        P(),
        P(),
        P(),
        P(),
        P("cell", None, None),
        P("cell", "net", None, None),
        P("cell", "net", None, None),
        P("cell", "net"),
    )
    return jax.shard_map(
        local,
        mesh=mesh,
        in_specs=placed,
        out_specs=(P(("cell", "net"), None), P(("cell", "net"), None), P(), P(), P(), P()),
        check_vma=False,
    )
```

```python
import functools

import jax
import jax.numpy as jnp
from jax import lax
from jax.experimental import pallas as pl
from jax.experimental.pallas import tpu as pltpu
from jax.sharding import PartitionSpec as P

NETS_BLK = 128
BF16 = jnp.bfloat16
F32 = jnp.float32
VMEM_LIMIT = 40 * 1024 * 1024


def dot_nn(a, b):
    return jnp.dot(a, b, preferred_element_type=F32)


def dot_nt(a, b):
    return lax.dot_general(a, b, (((1,), (1,)), ((), ())), preferred_element_type=F32)


def dot_tn(a, b):
    return lax.dot_general(a, b, (((0,), (0,)), ((), ())), preferred_element_type=F32)


def pick_ids(idx, part_of, slot_of):
    parts, slots = idx.shape
    lanes = part_of.shape[1]
    spread = (lax.broadcasted_iota(jnp.int32, (slots, lanes), 0) == slot_of).astype(BF16)
    high = dot_nn((idx >> 6).astype(F32).astype(BF16), spread)
    low = dot_nn((idx & 63).astype(F32).astype(BF16), spread)
    mine = lax.broadcasted_iota(jnp.int32, (parts, lanes), 0) == part_of
    return jnp.sum(jnp.where(mine, high * 64.0 + low, 0.0), axis=0, keepdims=True).astype(jnp.int32)


def slot_onehot(idx, cells):
    parts, slots = idx.shape
    lane = lax.broadcasted_iota(jnp.int32, (1, parts * slots), 1)
    return row_onehot(cells, pick_ids(idx, lane // slots, lane % slots))


def start_copies(pairs, sems):
    copies = [pltpu.make_async_copy(src, dst, sems.at[i]) for i, (src, dst) in enumerate(pairs)]
    for copy in copies:
        copy.start()
    return copies


def gather_kernel(fast, pos_ref, count_ref, idx_hbm, x_hbm, g_hbm, net_hbm, ref_hbm, ints_ref, *rest):
    *outs, idx_ref, x_ref, g_ref, net_ref, ref_ref, sems = rest
    copies = start_copies(
        [(idx_hbm, idx_ref), (x_hbm, x_ref), (g_hbm, g_ref), (net_hbm, net_ref), (ref_hbm, ref_ref)], sems
    )
    for copy in copies:
        copy.wait()
    slot_max = net_ref.shape[2]
    ints_ref[0] = jnp.broadcast_to(count_ref[...], ints_ref.shape[1:])
    ints_ref[0, :slot_max, :] = net_ref[0, 0]
    ints_ref[0, slot_max : 2 * slot_max, :] = ref_ref[0, 0]
    part_count, slots = idx_ref.shape[1:]
    cells, feat = x_ref.shape
    if fast:
        order = [pos_ref[0] ^ bits for bits in (0, 2, 4, 6, 1, 3, 5, 7)]
        idx = jnp.concatenate([idx_ref[0, pl.ds(part, 1), :] for part in order], axis=0)
        onehot = slot_onehot(idx, cells)
        for at, values in ((0, x_ref), (feat, g_ref)):
            rows = dot_tn(onehot, values[...]).astype(BF16)
            for half, out_ref in enumerate(outs):
                out_ref[:, :, at : at + feat] = rows[64 * half : 64 * (half + 1)].reshape(4, slots, feat)
        return
    (out_ref,) = outs
    group = 128 // slots
    for first in range(0, part_count, group):
        onehot = slot_onehot(idx_ref[0, first : first + group], cells)
        for at, values in ((0, x_ref), (feat, g_ref)):
            rows = dot_tn(onehot, values[...]).astype(BF16)
            out_ref[first : first + group, :, at : at + feat] = rows.reshape(group, slots, feat)


def split_bf16(x):
    high = x.astype(BF16)
    return high, (x - high.astype(F32)).astype(BF16)


def block_ids(ints_refs):
    nets, refs = [], []
    pins = ints_refs[0].shape[2]
    extra_net = jnp.zeros((1, pins), jnp.int32)
    extra_ref = jnp.zeros((1, pins), jnp.int32)
    for ints in [ref[i] for ref in ints_refs for i in range(ref.shape[0])]:
        nets.append(ints[0:1, :])
        refs.append(ints[2:3, :])
        second = ints[4:5, :] > 1
        extra_net += jnp.where(second, ints[1:2, :] + 1, 0)
        extra_ref += jnp.where(second, ints[3:4, :] + 1, 0)
    nets.append(extra_net - 1)
    refs.append(extra_ref - 1)
    return nets, refs


def row_onehot(rows, ids):
    return (lax.broadcasted_iota(jnp.int32, (rows, ids.shape[1]), 0) == ids).astype(BF16)


def column_onehot(ids, lanes):
    return (lax.broadcasted_iota(jnp.int32, (ids.shape[0], lanes), 1) == ids).astype(BF16)


def tiled_columns(ids, length):
    low = column_onehot(ids & 127, 128)
    high = jnp.broadcast_to((ids >> 7).astype(F32).astype(BF16), low.shape)
    return [jnp.where(high == t, low, jnp.zeros((), BF16)) for t in range(length // 128)]


def tiled_rows(ids, length):
    low = row_onehot(128, ids & 127)
    high = jnp.broadcast_to((ids >> 7).astype(F32).astype(BF16), low.shape)
    return [jnp.where(high == t, low, jnp.zeros((), BF16)) for t in range(length // 128)]


def net_inverse(pin_net):
    return 1.0 / jnp.maximum(jnp.sum(pin_net.astype(F32), axis=1, keepdims=True), 1.0)


def id_columns(ids, wide):
    wide[...] = jnp.zeros_like(wide)
    wide[:16, :] = ids[...]
    return wide[...].T.astype(jnp.int32)


def spread_kernel(fast, slots, pos_ref, *refs):
    ints_refs, refs = refs[:-18], refs[-18:]
    w_in_hbm, w_net_hbm, bias_hbm, w_out_hbm, ids_hbm, *refs = refs
    at_pin, at_row, net_pin, pin_net, edge_pin, w_in_ref, w_net_ref, bias_ref, w_out_ref, *refs = refs
    ids, wide, sems, out_sem = refs
    cells = at_pin.shape[1]
    hid = w_in_ref.shape[1]
    pins = ids.shape[1]
    table_len = at_row.shape[0]
    mine = pl.ds(pl.multiple_of(pos_ref[1] * hid, hid), hid)
    copies = start_copies(
        [
            (w_in_hbm.at[:, mine], w_in_ref),
            (w_net_hbm.at[:, mine], w_net_ref),
            (bias_hbm.at[:, mine], bias_ref),
            (w_out_hbm.at[mine, :], w_out_ref),
        ],
        sems,
    )
    nets, refs = block_ids(ints_refs)
    blocks = len(nets)
    if fast:
        refs = [jnp.where(row < cells, row, ((row - cells) ^ (pos_ref[0] * slots)) + cells) for row in refs]
    ids[...] = jnp.zeros_like(ids)
    for b in range(blocks):
        ids[b : b + 1, :] = nets[b].astype(F32)
        ids[8 + b : 9 + b, :] = refs[b].astype(F32)
    outgoing = pltpu.make_async_copy(ids, ids_hbm, out_sem)
    outgoing.start()
    columns = id_columns(ids, wide)
    for b in range(blocks):
        of = slice(b * pins, (b + 1) * pins)
        as_columns, as_rows = tiled_columns(columns[:, 8 + b : 9 + b], table_len), tiled_rows(refs[b], table_len)
        for t, (tile_column, tile_row) in enumerate(zip(as_columns, as_rows)):
            if t < cells // 128:
                at_pin[of, t * 128 : (t + 1) * 128] = tile_column
            else:
                edge_pin[of, t * 128 - cells : (t + 1) * 128 - cells] = tile_column
            at_row[t * 128 : (t + 1) * 128, of] = tile_row
        net_pin[of, :] = column_onehot(columns[:, b : b + 1], NETS_BLK)
        pin_net[:, of] = row_onehot(NETS_BLK, nets[b])
    for copy in copies:
        copy.wait()
    outgoing.wait()


def own_pins_kernel(after_ref, at_pin, x_hbm, g_hbm, taken, table, sems):
    feat = x_hbm.shape[1]
    copies = start_copies([(x_hbm, table.at[:, :feat]), (g_hbm, table.at[:, feat:])], sems)
    for copy in copies:
        copy.wait()
    taken[...] = dot_nn(at_pin[...], table[...]).astype(BF16)


def layer_kernel(fast, halos, *refs):
    halo_refs, refs = refs[:halos], refs[halos:]
    at_row, net_pin, pin_net, edge_pin, w_in_ref, w_net_ref, bias_ref, w_out_ref, local_taken, *refs = refs
    x_hbm, g_hbm, grads_ref, sums_hbm, net_grads_hbm, *refs = refs
    table, sems, sums, net_grads, out_sems, taken, net_feats, terms = refs
    cells, feat = x_hbm.shape
    hid = w_in_ref.shape[1]
    table_len, pin_count = at_row.shape
    blocks = net_grads.shape[0] // NETS_BLK
    pins = pin_count // blocks
    copies = start_copies([(x_hbm, table.at[:cells, :feat]), (g_hbm, table.at[:cells, feat:])], sems)
    at = cells
    for ref in halo_refs:
        for part in range(ref.shape[0]):
            table[at : at + ref.shape[1], :] = ref[part]
            at += ref.shape[1]
    for b in range(blocks):
        of = slice(b * pins, (b + 1) * pins)
        nets_of = slice(b * NETS_BLK, (b + 1) * NETS_BLK)
        edge = dot_nn(edge_pin[of, :], table[cells:, :])
        taken[of, :] = (edge + local_taken[of, :].astype(F32)).astype(BF16)
        net_sum = dot_nn(pin_net[:, of], taken[of, :feat])
        net_feats[nets_of, :] = (net_sum * net_inverse(pin_net[:, of])).astype(BF16)
    net_pre = dot_nn(net_feats[...], w_net_ref[...]).astype(BF16)
    scale = 0.7978845608028654
    for b in range(blocks):
        of = slice(b * pins, (b + 1) * pins)
        nets_of = slice(b * NETS_BLK, (b + 1) * NETS_BLK)
        pre = dot_nn(taken[of, :feat], w_in_ref[...]) + dot_nn(net_pin[of, :], net_pre[nets_of]) + bias_ref[...]
        pulled = dot_nt(taken[of, feat:], w_out_ref[...])
        square = pre * pre
        bend = jnp.tanh(pre * (scale + (scale * 0.044715) * square))
        half = 0.5 * bend + 0.5
        terms[of, :hid] = (pre * half).astype(BF16)
        slope = half + (0.5 * pre) * (1.0 - bend * bend) * (scale + (3 * scale * 0.044715) * square)
        pre_grad = (pulled * slope).astype(BF16)
        terms[of, hid:] = pre_grad
        net_grads[nets_of, :] = dot_nn(pin_net[:, of], pre_grad).astype(BF16)
    sums[...] = dot_nn(at_row[...], terms[...])
    outgoing = start_copies([(sums, sums_hbm), (net_grads, net_grads_hbm)], out_sems)
    hidden_high, hidden_low = split_bf16(sums[:, :hid])
    grad_high, grad_low = split_bf16(sums[:, hid:])
    for copy in copies:
        copy.wait()
    table_x, table_g = table[:, :feat], table[:, feat:]
    acc_in = dot_tn(table_x, grad_high) + dot_tn(table_x, grad_low)
    acc_out = dot_tn(hidden_high, table_g) + dot_tn(hidden_low, table_g)
    acc_net = dot_tn(net_feats[...], net_grads[...])
    acc_bias = jnp.broadcast_to(jnp.sum(sums[:, hid:], axis=0, keepdims=True), (8, hid))
    if fast:
        part_count, rows, _ = grads_ref.shape
        part = feat // part_count
        for to in range(part_count):
            of = slice(to * part, (to + 1) * part)
            blocks_of = [acc_in[of, :], acc_net[of, :], acc_out[of, :], acc_bias]
            grads_ref[to] = jnp.concatenate([x.astype(BF16) for x in blocks_of], axis=0)
    else:
        grads_ref[:feat, :] = acc_in
        grads_ref[feat : 2 * feat, :] = acc_net
        grads_ref[2 * feat : 2 * feat + hid, :] = acc_out
        grads_ref[2 * feat + hid :, :] = acc_bias
    for copy in outgoing:
        copy.wait()


def back_kernel(fast, pos_ref, ids_hbm, sums_hbm, net_grads_hbm, w_in_hbm, w_net_hbm, w_out_hbm, *rest):
    *outs, ids, wide, sums, net_grads, w_in_ref, w_net_ref, w_out_ref, sems, at_row, net_backs, acc = rest
    table_len = acc.shape[0]
    feat, hid = w_in_ref.shape
    blocks = net_grads.shape[0] // NETS_BLK
    pins = ids.shape[1]
    mine = pl.ds(pl.multiple_of(pos_ref[1] * hid, hid), hid)
    copies = start_copies(
        [
            (ids_hbm, ids),
            (net_grads_hbm, net_grads),
            (w_net_hbm.at[:, mine], w_net_ref),
            (w_in_hbm.at[:, mine], w_in_ref),
            (w_out_hbm.at[mine, :], w_out_ref),
            (sums_hbm, sums),
        ],
        sems,
    )
    copies[0].wait()
    columns = id_columns(ids, wide)
    rows = ids[...].astype(jnp.int32)
    for b in range(blocks):
        of = slice(b * pins, (b + 1) * pins)
        for t, tile in enumerate(tiled_rows(rows[8 + b : 9 + b, :], table_len)):
            at_row[t * 128 : (t + 1) * 128, of] = tile
    for copy in copies[1:3]:
        copy.wait()
    for b in range(blocks):
        of = slice(b * pins, (b + 1) * pins)
        nets_of = slice(b * NETS_BLK, (b + 1) * NETS_BLK)
        inverse = net_inverse(row_onehot(NETS_BLK, rows[b : b + 1, :]))
        feat_grad = (dot_nt(net_grads[nets_of, :], w_net_ref[...]) * inverse).astype(BF16)
        net_backs[of, :] = dot_nn(column_onehot(columns[:, b : b + 1], NETS_BLK), feat_grad).astype(BF16)
    for copy in copies[3:]:
        copy.wait()
    hidden_high, hidden_low = split_bf16(sums[:, :hid])
    grad_high, grad_low = split_bf16(sums[:, hid:])
    acc[:, :feat] = dot_nn(hidden_high, w_out_ref[...]) + dot_nn(hidden_low, w_out_ref[...])
    acc[:, feat:] = (
        dot_nt(grad_high, w_in_ref[...]) + dot_nt(grad_low, w_in_ref[...]) + dot_nn(at_row[...], net_backs[...])
    )
    if fast:
        own_ref, far_ref, twin_ref = outs
        length = own_ref.shape[0]
        cells = table_len - 128
        share = cells // 4
        edges = acc[cells:, :].astype(BF16)
        row = lax.broadcasted_iota(jnp.int32, (length - share, 128), 0)
        lane = lax.broadcasted_iota(jnp.int32, row.shape, 1)
        for bits, ref, at in ((0, own_ref, 0), (2, far_ref, 0), (1, twin_ref, 0), (3, twin_ref, length)):
            to = pos_ref[1] ^ bits
            rows = acc[pl.ds(pl.multiple_of(to * share, share), share), :]
            ref[at : at + share, :] = rows.astype(ref.dtype)
            of = lane == ((row >> 2) * 16 + to * 4 + (row & 3))
            ref[at + share : at + length, :] = dot_nn(of.astype(BF16), edges).astype(ref.dtype)
        return
    own_ref, send_ref = outs
    cells = own_ref.shape[0]
    own_ref[...] = acc[:cells, :]
    part_count, rows, _ = send_ref.shape
    slots = rows // 2
    for part in range(part_count):
        of = slice(cells + part * slots, cells + (part + 1) * slots)
        send_ref[part, :slots, :] = acc[of, :feat].astype(BF16)
        send_ref[part, slots:, :] = acc[of, feat:].astype(BF16)


def pair_kernel(own_ref, far_ref, twin_ref, own_sum_ref, far_sum_ref):
    length = own_ref.shape[0]
    own_sum_ref[...] = own_ref[...] + twin_ref[:length, :].astype(F32)
    far_sum_ref[...] = (far_ref[...] + twin_ref[length:, :].astype(F32)).astype(BF16)


def sum_kernel(got_ref, own_ref, *rest):
    far_ref, *payloads, rows_ref, bias_ref = rest
    total = own_ref[...] + far_ref[...].astype(F32)
    share, wide = rows_ref.shape
    feat = wide // 2
    rows_ref[...] = total[:share]
    piece = got_ref[0].astype(F32)
    for part in range(1, got_ref.shape[0]):
        piece += got_ref[part].astype(F32)
    rows = piece.shape[0] - 8
    bias_ref[...] = jnp.concatenate([piece[rows:]] * 2, axis=0).astype(BF16)
    for k, payload in enumerate(payloads):
        edges = []
        for odd in range(2):
            at = share + 4 * (2 * k + odd)
            edges += [total[at : at + 4, :feat], total[at : at + 4, feat:]]
        payload[...] = jnp.concatenate([piece[:rows]] + edges, axis=0).astype(BF16)


def place(pos_ref, parts, outs, buffer, sems):
    rows, hid = buffer.shape[1:]
    part = rows // 3
    copies = []
    for at, (ref, start, cell_bits, net_bits) in enumerate(parts):
        row = pl.multiple_of((pos_ref[0] ^ cell_bits) * part, part)
        first = pl.multiple_of((pos_ref[1] ^ net_bits) * hid, hid)
        buffer[at] = ref[start : start + rows, :].astype(F32)
        targets = [
            outs[0].at[pl.ds(row, part), pl.ds(first, hid)],
            outs[1].at[pl.ds(row, part), pl.ds(first, hid)],
            outs[2].at[pl.ds(pl.multiple_of(first + row, part), part), :],
        ]
        for matrix, target in enumerate(targets):
            source = buffer.at[at, matrix * part : (matrix + 1) * part, :]
            copies.append(pltpu.make_async_copy(source, target, sems.at[3 * at + matrix]))
            copies[-1].start()
    return copies


def place_kernel(tags, olds, pos_ref, *refs):
    ins, refs = refs[: len(tags)], refs[len(tags) + olds :]
    outs, (buffer, sems) = refs[:3], refs[3:]
    parts = [(ref,) + tag for ref, some in zip(ins, tags) for tag in some]
    for copy in place(pos_ref, parts, outs, buffer, sems):
        copy.wait()


def edge_rows(edges):
    return jnp.concatenate([edge[:64, :] for edge in edges], axis=0)


def first_kernel(tags, pos_ref, idx_ref, x_hbm, g_hbm, rows_ref, *refs):
    ins, refs = refs[: len(tags)], refs[len(tags) :]
    edges, refs = refs[:2], refs[2:]
    grads, (total_ref, pick_y_ref, pick_x_ref, buffer, sems, x_ref, g_ref, row_sems) = refs[:3], refs[3:]
    share, wide = rows_ref.shape
    feat = wide // 2
    cell, net = pos_ref[0], pos_ref[1]
    mine = pl.ds(pl.multiple_of(net * share, share), share)
    copies = start_copies([(x_hbm.at[mine, :], x_ref), (g_hbm.at[mine, :], g_ref)], row_sems)
    parts = [(ref,) + tag for ref, some in zip(ins, tags) for tag in some]
    placed = place(pos_ref, parts, grads, buffer, sems)
    lane = lax.broadcasted_iota(jnp.int32, (1, 256), 1)
    bits, source, is_back, slot = lane >> 6, (lane >> 3) & 7, (lane >> 2) & 1, lane & 3
    part_of = cell ^ (((source & 3) << 1) | (source >> 2))
    ids = pick_ids(idx_ref[0], part_of, ((net ^ bits) << 2) | slot) - net * share
    pick_y = row_onehot(share, jnp.where(is_back == 0, ids, -1))
    pick_x = row_onehot(share, jnp.where(is_back == 1, ids, -1))
    pick_y_ref[...] = pick_y[:, 128:]
    pick_x_ref[...] = pick_x[:, 128:]
    halo = edge_rows(edges)
    for copy in copies:
        copy.wait()
    total_ref[:, :feat] = x_ref[...].astype(F32) + rows_ref[:, :feat] + dot_nn(pick_y[:, :128], halo)
    total_ref[:, feat:] = g_ref[...].astype(F32) + rows_ref[:, feat:] + dot_nn(pick_x[:, :128], halo)
    for copy in placed:
        copy.wait()


def finish_kernel(tags, pos_ref, total_ref, pick_y_ref, pick_x_ref, *refs):
    ins, refs = refs[: len(tags)], refs[len(tags) :]
    edges, refs = refs[:4], refs[4 + 3 :]
    grads, (updated_ref, back_ref, bias_ref, buffer, sems) = refs[:3], refs[3:]
    feat = updated_ref.shape[1]
    parts = [(ref,) + tag for ref, some in zip(ins, tags) for tag in some]
    placed = place(pos_ref, parts, grads, buffer, sems)
    halo = edge_rows(edges[2:])
    updated_ref[...] = (total_ref[:, :feat] + dot_nn(pick_y_ref[...], halo)).astype(BF16)
    back_ref[...] = (total_ref[:, feat:] + dot_nn(pick_x_ref[...], halo)).astype(BF16)
    for bits, edge in enumerate(edges):
        at = pl.multiple_of((pos_ref[1] ^ bits) * feat, feat)
        bias_ref[:, pl.ds(at, feat)] = edge[64:, :].astype(F32)[:1]
    for copy in placed:
        copy.wait()


def combine_kernel(pos_ref, idx_ref, got_ref, own_ref, *outs):
    part_count, slots = idx_ref.shape[1:]
    cells, wide = own_ref.shape
    feat = wide // 2
    group = 128 // slots
    rows_y = own_ref[:, :feat]
    rows_x = own_ref[:, feat:]
    for first in range(0, part_count, group):
        onehot = slot_onehot(idx_ref[0, first : first + group], cells)
        y = got_ref[first : first + group, :slots, :].reshape(128, feat)
        x = got_ref[first : first + group, slots:, :].reshape(128, feat)
        rows_y += dot_nn(onehot, y)
        rows_x += dot_nn(onehot, x)
    *shares, scratch = outs
    scratch[:, :feat] = rows_y
    scratch[:, feat:] = rows_x
    share = cells // len(shares)
    for bits, share_ref in enumerate(shares):
        at = pl.multiple_of((pos_ref[1] ^ bits) * share, share)
        share_ref[...] = scratch[pl.ds(at, share), :].astype(share_ref.dtype)


def plain_rows_kernel(pos_ref, x_hbm, g_hbm, own_ref, *rest):
    *others, updated_ref, back_ref, x_ref, g_ref, sems = rest
    share, feat = updated_ref.shape
    mine = pl.ds(pl.multiple_of(pos_ref[1] * share, share), share)
    copies = start_copies([(x_hbm.at[mine, :], x_ref), (g_hbm.at[mine, :], g_ref)], sems)
    total = own_ref[...]
    for other in others:
        total += other[...].astype(F32)
    for copy in copies:
        copy.wait()
    updated_ref[...] = (x_ref[...].astype(F32) + total[:, :feat]).astype(BF16)
    back_ref[...] = (g_ref[...].astype(F32) + total[:, feat:]).astype(BF16)


def whole(count):
    return [pl.BlockSpec(memory_space=pltpu.VMEM)] * count


SMEM = pl.BlockSpec(memory_space=pltpu.SMEM)
HBM = pl.BlockSpec(memory_space=pltpu.HBM)
PARAMS = dict(compiler_params=pltpu.CompilerParams(vmem_limit_bytes=VMEM_LIMIT))


def about(microseconds):
    return pl.CostEstimate(flops=0, transcendentals=0, bytes_accessed=int(microseconds * 3.6e6))


def in_hbm(*arrays):
    return [pltpu.with_memory_space_constraint(x, pltpu.HBM) for x in arrays]


def flip(x, axis, bits):
    size = lax.axis_size(axis)
    return lax.ppermute(x, axis, [(i, i ^ bits) for i in range(size)])


def both(x, cell_bits, net_bits):
    parts, group = lax.axis_size("cell"), lax.axis_size("net")
    pairs = [
        (c * group + n, (c ^ cell_bits(n)) * group + (n ^ net_bits)) for c in range(parts) for n in range(group)
    ]
    return lax.ppermute(x, ("cell", "net"), pairs)


def local(cell_feat, out_grad, w_in, w_net, bias, w_out, send_idx, pin_net, pin_ref, block_count):
    part_count = lax.axis_size("cell")
    group_size = lax.axis_size("net")
    cells, feat = cell_feat.shape
    hidden_dim = w_in.shape[1]
    hid = hidden_dim // group_size
    slots = send_idx.shape[2]
    pins = pin_net.shape[3]
    table_len = cells + part_count * slots
    fast = part_count == 8 and group_size == 4
    pos = jnp.stack([lax.axis_index("cell"), lax.axis_index("net")]).astype(jnp.int32)

    def shape(dtype, *dims):
        return jax.ShapeDtypeStruct(dims, dtype)

    if fast:
        sent_shape = [shape(BF16, 4, slots, 2 * feat)] * 2
    else:
        sent_shape = [shape(BF16, part_count, slots, 2 * feat)]
    ints, *sent = pl.pallas_call(
        functools.partial(gather_kernel, fast),
        in_specs=[SMEM] + whole(1) + [HBM] * 5,
        out_specs=whole(1 + len(sent_shape)),
        out_shape=[shape(jnp.int32, 1, 8, pins)] + sent_shape,
        scratch_shapes=[
            pltpu.VMEM(send_idx.shape, jnp.int32),
            pltpu.VMEM((cells, feat), BF16),
            pltpu.VMEM((cells, feat), BF16),
            pltpu.VMEM(pin_net.shape, jnp.int32),
            pltpu.VMEM(pin_ref.shape, jnp.int32),
            pltpu.SemaphoreType.DMA((5,)),
        ],
        name="take_boundary",
        cost_estimate=about(2.0),
        **PARAMS,
    )(pos, block_count, *in_hbm(send_idx, cell_feat, out_grad, pin_net, pin_ref))
    if fast:
        keep, cross = sent
        all_ints = [ints] + [flip(ints, "net", bits) for bits in range(1, group_size)]
        cross = flip(cross, "cell", 1)
        near = [jnp.stack([keep[k], cross[k]]) for k in range(4)]
        near, all_ints = lax.optimization_barrier((near, all_ints))
        halo = [near[0]] + [flip(near[k], "cell", 2 * k) for k in (1, 2, 3)]
    else:
        halo = [lax.all_to_all(sent[0], "cell", split_axis=0, concat_axis=0, tiled=True)]
        all_ints = [lax.all_gather(ints, "net", tiled=True)]

    blocks = group_size + 1
    part = feat // part_count
    share = cells // group_size
    edge = part_count * slots // group_size
    all_pins = blocks * pins
    spread_shape = [
        shape(BF16, all_pins, cells),
        shape(BF16, table_len, all_pins),
        shape(BF16, all_pins, NETS_BLK),
        shape(BF16, NETS_BLK, all_pins),
        shape(BF16, all_pins, table_len - cells),
        shape(BF16, feat, hid),
        shape(BF16, feat, hid),
        shape(F32, 1, hid),
        shape(BF16, hid, feat),
    ]
    ids, at_pin, *spread = pl.pallas_call(
        functools.partial(spread_kernel, fast, slots),
        in_specs=[SMEM] + whole(len(all_ints)) + [HBM] * 4,
        out_specs=[HBM] + whole(9),
        out_shape=[pltpu.HBM((16, pins), F32)] + spread_shape,
        scratch_shapes=[
            pltpu.VMEM((16, pins), F32),
            pltpu.VMEM((128, pins), F32),
            pltpu.SemaphoreType.DMA((4,)),
            pltpu.SemaphoreType.DMA,
        ],
        name="spread",
        cost_estimate=about(4.5),
        **PARAMS,
    )(pos, *all_ints, *in_hbm(w_in, w_net, bias.reshape(1, hidden_dim), w_out))
    taken = pl.pallas_call(
        own_pins_kernel,
        in_specs=[pl.BlockSpec(memory_space=pl.ANY)] + whole(1) + [HBM] * 2,
        out_specs=whole(1)[0],
        out_shape=shape(BF16, all_pins, 2 * feat),
        scratch_shapes=[pltpu.VMEM((cells, 2 * feat), BF16), pltpu.SemaphoreType.DMA((2,))],
        name="own_pins",
        cost_estimate=about(2.5),
        **PARAMS,
    )(halo[0], at_pin, *in_hbm(cell_feat, out_grad))

    grads, sums, net_grads = pl.pallas_call(
        functools.partial(layer_kernel, fast, len(halo)),
        in_specs=whole(len(halo) + 9) + [HBM] * 2,
        out_specs=whole(1) + [HBM] * 2,
        out_shape=[
            shape(BF16, part_count, 3 * part + 8, feat) if fast else shape(F32, 2 * feat + hid + 8, hid),
            pltpu.HBM((table_len, 2 * hid), F32),
            pltpu.HBM((blocks * NETS_BLK, hid), BF16),
        ],
        scratch_shapes=[
            pltpu.VMEM((table_len, 2 * feat), BF16),
            pltpu.SemaphoreType.DMA((2,)),
            pltpu.VMEM((table_len, 2 * hid), F32),
            pltpu.VMEM((blocks * NETS_BLK, hid), BF16),
            pltpu.SemaphoreType.DMA((2,)),
            pltpu.VMEM((all_pins, 2 * feat), BF16),
            pltpu.VMEM((blocks * NETS_BLK, feat), BF16),
            pltpu.VMEM((all_pins, 2 * hid), BF16),
        ],
        name="layer",
        cost_estimate=about(7.7),
        **PARAMS,
    )(*halo, *spread, taken, *in_hbm(cell_feat, out_grad))

    if fast:
        got = lax.all_to_all(grads, "cell", split_axis=0, concat_axis=0, tiled=True)
        length = share + edge
        out_shape = [shape(F32, length, 2 * feat)] * 2 + [shape(BF16, 2 * length, 2 * feat)]
    else:
        out_shape = [shape(F32, cells, 2 * feat), shape(BF16, part_count, 2 * slots, feat)]
    outs = pl.pallas_call(
        functools.partial(back_kernel, fast),
        in_specs=[SMEM] + [HBM] * 6,
        out_specs=whole(len(out_shape)),
        out_shape=out_shape,
        scratch_shapes=[
            pltpu.VMEM((16, pins), F32),
            pltpu.VMEM((128, pins), F32),
            pltpu.VMEM((table_len, 2 * hid), F32),
            pltpu.VMEM((blocks * NETS_BLK, hid), BF16),
            pltpu.VMEM((feat, hid), BF16),
            pltpu.VMEM((feat, hid), BF16),
            pltpu.VMEM((hid, feat), BF16),
            pltpu.SemaphoreType.DMA((6,)),
            pltpu.VMEM((table_len, blocks * pins), BF16),
            pltpu.VMEM((blocks * pins, feat), BF16),
            pltpu.VMEM((table_len, 2 * feat), F32),
        ],
        name="back",
        cost_estimate=about(4.6),
        **PARAMS,
    )(pos, *in_hbm(ids, sums, net_grads, w_in, w_net, w_out))

    row_shapes = [shape(BF16, share, feat)] * 2
    row_scratch = [
        pltpu.VMEM((share, feat), BF16),
        pltpu.VMEM((share, feat), BF16),
        pltpu.SemaphoreType.DMA((2,)),
    ]
    grad_shapes = [shape(F32, feat, hidden_dim), shape(F32, feat, hidden_dim), shape(F32, hidden_dim, feat)]
    if not fast:
        own, send = outs
        got = lax.all_to_all(send, "cell", split_axis=0, concat_axis=0, tiled=True)
        shares = pl.pallas_call(
            combine_kernel,
            in_specs=[SMEM] + whole(3),
            out_specs=whole(group_size),
            out_shape=[shape(BF16 if bits else F32, share, 2 * feat) for bits in range(group_size)],
            scratch_shapes=[pltpu.VMEM((cells, 2 * feat), F32)],
            name="combine",
            **PARAMS,
        )(pos, send_idx, got, own)
        others = [flip(shares[bits], "net", bits) for bits in range(1, group_size)]
        updated, cell_grad = pl.pallas_call(
            plain_rows_kernel,
            in_specs=[SMEM] + [HBM] * 2 + whole(group_size),
            out_specs=whole(2),
            out_shape=row_shapes,
            scratch_shapes=row_scratch,
            name="own_rows",
            **PARAMS,
        )(pos, *in_hbm(cell_feat, out_grad), shares[0], *others)
        summed = lax.all_gather(lax.psum(grads, "cell"), "net")
        grad_in = jnp.moveaxis(summed[:, :feat], 0, 1).reshape(feat, hidden_dim)
        grad_net = jnp.moveaxis(summed[:, feat : 2 * feat], 0, 1).reshape(feat, hidden_dim)
        grad_out = summed[:, 2 * feat : 2 * feat + hid].reshape(hidden_dim, feat)
        grad_bias = summed[:, 2 * feat + hid].reshape(hidden_dim)
        return (updated, cell_grad, grad_in, grad_net, grad_bias, grad_out)

    own, far, twin_share = outs
    own, far = pl.pallas_call(
        pair_kernel,
        in_specs=whole(3),
        out_specs=whole(2),
        out_shape=[shape(F32, length, 2 * feat), shape(BF16, length, 2 * feat)],
        name="pairs",
        **PARAMS,
    )(own, far, flip(twin_share, "net", 1))
    rows_of = 3 * part
    *pays, rows, bias_sum = pl.pallas_call(
        sum_kernel,
        in_specs=whole(3),
        out_specs=whole(6),
        out_shape=[shape(BF16, rows_of + 16, feat)] * 4 + [shape(F32, share, 2 * feat), shape(BF16, 16, feat)],
        name="sums",
        cost_estimate=about(0.2),
        **PARAMS,
    )(got, own, flip(far, "net", 2))
    near = [pays[0]] + [flip(pays[k], "cell", 2 * k) for k in (1, 2, 3)]
    across = flip(jnp.concatenate(near[:2] + [a[rows_of:] for a in near[2:]]), "cell", 1)
    second = jnp.concatenate([a[:rows_of] for a in near[2:]])
    second = jnp.concatenate([second, flip(second, "net", 2)])
    starts = [rows_of, 2 * rows_of + 16, 2 * rows_of + 32, 2 * rows_of + 48]
    edges = [a[rows_of : rows_of + 8] for a in near] + [across[at + 8 : at + 16] for at in starts]
    full = rows_of + 16
    pieces = [near[0][:rows_of], near[1][:rows_of], across[:rows_of], across[full : full + rows_of]]
    first = jnp.concatenate(pieces + edges + [bias_sum])
    early = [flip(first, "net", 1), flip(second, "net", 1)]
    third, fourth = flip(first, "net", 2), flip(second, "cell", 1)
    first_tag = [(0, 0, 0), (rows_of, 2, 0), (2 * rows_of, 1, 0), (3 * rows_of, 3, 0)]
    second_tag = [(0, 4, 0), (rows_of, 6, 0), (2 * rows_of, 4, 2), (3 * rows_of, 6, 2)]
    early_tags = [first_tag, second_tag]
    late_tags = [[(at, c, n ^ 2) for at, c, n in first_tag], [(at, c ^ 1, n) for at, c, n in second_tag]]

    def twin(tags):
        return [[(at, c, n ^ 1) for at, c, n in tag] for tag in tags]

    def scratch(arrays):
        return [pltpu.VMEM((4 * len(arrays), rows_of, hid), F32), pltpu.SemaphoreType.DMA((12 * len(arrays),))]

    *grads, total, pick_y, pick_x = pl.pallas_call(
        functools.partial(first_kernel, early_tags + twin(early_tags)),
        in_specs=[SMEM] + whole(1) + [HBM] * 2 + whole(1 + 4 + 2),
        out_specs=[HBM] * 3 + whole(3),
        out_shape=grad_shapes + [shape(F32, share, 2 * feat)] + [shape(BF16, share, 128)] * 2,
        scratch_shapes=scratch([0] * 4) + row_scratch,
        name="first_pieces",
        **PARAMS,
    )(pos, send_idx, *in_hbm(cell_feat, out_grad), rows, first, second, *early, first[4 * rows_of :], early[0][4 * rows_of :])
    third, fourth, grads = lax.optimization_barrier((third, fourth, grads))
    late = [flip(third, "net", 1), flip(fourth, "net", 1)]
    grads = pl.pallas_call(
        functools.partial(place_kernel, late_tags, 3),
        in_specs=[SMEM] + whole(2) + [HBM] * 3,
        out_specs=[HBM] * 3,
        out_shape=grad_shapes,
        scratch_shapes=scratch(late),
        input_output_aliases={3 + i: i for i in range(3)},
        name="place",
        **PARAMS,
    )(pos, third, fourth, *grads)
    all_edges = [a[4 * rows_of :] for a in (first, early[0], third, late[0])]
    grad_in, grad_net, grad_out, updated, cell_grad, grad_bias = pl.pallas_call(
        functools.partial(finish_kernel, twin(late_tags)),
        in_specs=[SMEM] + whole(3 + 2 + 4) + [HBM] * 3,
        out_specs=[HBM] * 3 + whole(3),
        out_shape=grad_shapes + row_shapes + [shape(F32, 1, hidden_dim)],
        scratch_shapes=scratch(late),
        input_output_aliases={4 + 2 + 4 + i: i for i in range(3)},
        name="finish",
        **PARAMS,
    )(pos, total, pick_y, pick_x, *late, *all_edges, *grads)
    return (updated, cell_grad, grad_in, grad_net, grad_bias.reshape(hidden_dim), grad_out)


def solution(mesh):
    placed = (
        P("cell", None),
        P("cell", None),
        P(),
        P(),
        P(),
        P(),
        P("cell", None, None),
        P("cell", "net", None, None),
        P("cell", "net", None, None),
        P("cell", "net"),
    )
    return jax.shard_map(
        local,
        mesh=mesh,
        in_specs=placed,
        out_specs=(P(("cell", "net"), None), P(("cell", "net"), None), P(), P(), P(), P()),
        check_vma=False,
    )
```

```python
import functools

import jax
import jax.numpy as jnp
from jax import lax
from jax.experimental import pallas as pl
from jax.experimental.pallas import tpu as pltpu
from jax.sharding import PartitionSpec as P

NETS_BLK = 128
BF16 = jnp.bfloat16
F32 = jnp.float32
VMEM_LIMIT = 40 * 1024 * 1024


def dot_nn(a, b):
    return jnp.dot(a, b, preferred_element_type=F32)


def dot_nt(a, b):
    return lax.dot_general(a, b, (((1,), (1,)), ((), ())), preferred_element_type=F32)


def dot_tn(a, b):
    return lax.dot_general(a, b, (((0,), (0,)), ((), ())), preferred_element_type=F32)


def pick_ids(idx, part_of, slot_of):
    parts, slots = idx.shape
    lanes = part_of.shape[1]
    spread = (lax.broadcasted_iota(jnp.int32, (slots, lanes), 0) == slot_of).astype(BF16)
    high = dot_nn((idx >> 6).astype(F32).astype(BF16), spread)
    low = dot_nn((idx & 63).astype(F32).astype(BF16), spread)
    mine = lax.broadcasted_iota(jnp.int32, (parts, lanes), 0) == part_of
    return jnp.sum(jnp.where(mine, high * 64.0 + low, 0.0), axis=0, keepdims=True).astype(jnp.int32)


def slot_onehot(idx, cells):
    parts, slots = idx.shape
    lane = lax.broadcasted_iota(jnp.int32, (1, parts * slots), 1)
    return row_onehot(cells, pick_ids(idx, lane // slots, lane % slots))


def start_copies(pairs, sems):
    copies = [pltpu.make_async_copy(src, dst, sems.at[i]) for i, (src, dst) in enumerate(pairs)]
    for copy in copies:
        copy.start()
    return copies


def gather_kernel(fast, count_ref, idx_hbm, x_hbm, g_hbm, net_hbm, ref_hbm, ints_ref, *rest):
    *outs, idx_ref, x_ref, g_ref, net_ref, ref_ref, sems = rest
    copies = start_copies(
        [(idx_hbm, idx_ref), (x_hbm, x_ref), (g_hbm, g_ref), (net_hbm, net_ref), (ref_hbm, ref_ref)], sems
    )
    for copy in copies:
        copy.wait()
    slot_max = net_ref.shape[2]
    ints_ref[0] = jnp.broadcast_to(count_ref[...], ints_ref.shape[1:])
    ints_ref[0, :slot_max, :] = net_ref[0, 0]
    ints_ref[0, slot_max : 2 * slot_max, :] = ref_ref[0, 0]
    part_count, slots = idx_ref.shape[1:]
    cells, feat = x_ref.shape
    if fast:
        cell = lax.axis_index("cell")
        order = [cell ^ bits for bits in range(part_count)]
        idx = jnp.concatenate([idx_ref[0, pl.ds(part, 1), :] for part in order], axis=0)
        onehot = slot_onehot(idx, cells)
        for at, values in ((0, x_ref), (feat, g_ref)):
            rows = dot_tn(onehot, values[...]).astype(BF16)
            for k, out_ref in enumerate(outs):
                out_ref[:, :, at : at + feat] = rows[32 * k : 32 * (k + 1)].reshape(2, slots, feat)
        return
    (out_ref,) = outs
    group = 128 // slots
    for first in range(0, part_count, group):
        onehot = slot_onehot(idx_ref[0, first : first + group], cells)
        for at, values in ((0, x_ref), (feat, g_ref)):
            rows = dot_tn(onehot, values[...]).astype(BF16)
            out_ref[first : first + group, :, at : at + feat] = rows.reshape(group, slots, feat)


def split_bf16(x):
    high = x.astype(BF16)
    return high, (x - high.astype(F32)).astype(BF16)


def block_ids(ints_refs):
    nets, refs = [], []
    pins = ints_refs[0].shape[2]
    extra_net = jnp.zeros((1, pins), jnp.int32)
    extra_ref = jnp.zeros((1, pins), jnp.int32)
    for ints in [ref[i] for ref in ints_refs for i in range(ref.shape[0])]:
        nets.append(ints[0:1, :])
        refs.append(ints[2:3, :])
        second = ints[4:5, :] > 1
        extra_net += jnp.where(second, ints[1:2, :] + 1, 0)
        extra_ref += jnp.where(second, ints[3:4, :] + 1, 0)
    nets.append(extra_net - 1)
    refs.append(extra_ref - 1)
    return nets, refs


def row_onehot(rows, ids):
    return (lax.broadcasted_iota(jnp.int32, (rows, ids.shape[1]), 0) == ids).astype(BF16)


def column_onehot(ids, lanes):
    return (lax.broadcasted_iota(jnp.int32, (ids.shape[0], lanes), 1) == ids).astype(BF16)


def tiled_columns(ids, length):
    low = column_onehot(ids & 127, 128)
    high = jnp.broadcast_to((ids >> 7).astype(F32).astype(BF16), low.shape)
    return [jnp.where(high == t, low, jnp.zeros((), BF16)) for t in range(length // 128)]


def tiled_rows(ids, length):
    low = row_onehot(128, ids & 127)
    high = jnp.broadcast_to((ids >> 7).astype(F32).astype(BF16), low.shape)
    return [jnp.where(high == t, low, jnp.zeros((), BF16)) for t in range(length // 128)]


def net_inverse(pin_net):
    return 1.0 / jnp.maximum(jnp.sum(pin_net.astype(F32), axis=1, keepdims=True), 1.0)


def id_columns(ids, wide):
    wide[...] = jnp.zeros_like(wide)
    wide[:16, :] = ids[...]
    return wide[...].T.astype(jnp.int32)


def spread_kernel(fast, slots, pos_ref, *refs):
    ints_refs, refs = refs[:-18], refs[-18:]
    w_in_hbm, w_net_hbm, bias_hbm, w_out_hbm, ids_hbm, *refs = refs
    at_pin, at_row, net_pin, pin_net, edge_pin, w_in_ref, w_net_ref, bias_ref, w_out_ref, *refs = refs
    ids, wide, sems, out_sem = refs
    cells = at_pin.shape[1]
    hid = w_in_ref.shape[1]
    pins = ids.shape[1]
    table_len = at_row.shape[0]
    mine = pl.ds(pl.multiple_of(pos_ref[1] * hid, hid), hid)
    copies = start_copies(
        [
            (w_in_hbm.at[:, mine], w_in_ref),
            (w_net_hbm.at[:, mine], w_net_ref),
            (bias_hbm.at[:, mine], bias_ref),
            (w_out_hbm.at[mine, :], w_out_ref),
        ],
        sems,
    )
    nets, refs = block_ids(ints_refs)
    blocks = len(nets)
    if fast:
        refs = [jnp.where(row < cells, row, ((row - cells) ^ (pos_ref[0] * slots)) + cells) for row in refs]
    ids[...] = jnp.zeros_like(ids)
    for b in range(blocks):
        ids[b : b + 1, :] = nets[b].astype(F32)
        ids[8 + b : 9 + b, :] = refs[b].astype(F32)
    outgoing = pltpu.make_async_copy(ids, ids_hbm, out_sem)
    outgoing.start()
    columns = id_columns(ids, wide)
    for b in range(blocks):
        of = slice(b * pins, (b + 1) * pins)
        as_columns, as_rows = tiled_columns(columns[:, 8 + b : 9 + b], table_len), tiled_rows(refs[b], table_len)
        for t, (tile_column, tile_row) in enumerate(zip(as_columns, as_rows)):
            if t < cells // 128:
                at_pin[of, t * 128 : (t + 1) * 128] = tile_column
            else:
                edge_pin[of, t * 128 - cells : (t + 1) * 128 - cells] = tile_column
            at_row[t * 128 : (t + 1) * 128, of] = tile_row
        net_pin[of, :] = column_onehot(columns[:, b : b + 1], NETS_BLK)
        pin_net[:, of] = row_onehot(NETS_BLK, nets[b])
    for copy in copies:
        copy.wait()
    outgoing.wait()


def own_pins_kernel(after_ref, at_pin, x_hbm, g_hbm, taken, table, sems):
    feat = x_hbm.shape[1]
    copies = start_copies([(x_hbm, table.at[:, :feat]), (g_hbm, table.at[:, feat:])], sems)
    for copy in copies:
        copy.wait()
    taken[...] = dot_nn(at_pin[...], table[...]).astype(BF16)


def layer_kernel(fast, halos, *refs):
    halo_refs, refs = refs[:halos], refs[halos:]
    at_row, net_pin, pin_net, edge_pin, w_in_ref, w_net_ref, bias_ref, w_out_ref, local_taken, *refs = refs
    x_hbm, g_hbm, grads_ref, sums_hbm, net_grads_hbm, *refs = refs
    table, sems, sums, net_grads, out_sems, taken, net_feats, terms = refs
    cells, feat = x_hbm.shape
    hid = w_in_ref.shape[1]
    table_len, pin_count = at_row.shape
    blocks = net_grads.shape[0] // NETS_BLK
    pins = pin_count // blocks
    copies = start_copies([(x_hbm, table.at[:cells, :feat]), (g_hbm, table.at[:cells, feat:])], sems)
    if fast:
        *near, cross = halo_refs
        blocks_of = [block for k, ref in enumerate(near) for block in (ref[0], cross[k])]
        table[cells:, :] = jnp.concatenate(blocks_of, axis=0)
    else:
        table[cells:, :] = halo_refs[0][...].reshape(table_len - cells, 2 * feat)
    for b in range(blocks):
        of = slice(b * pins, (b + 1) * pins)
        nets_of = slice(b * NETS_BLK, (b + 1) * NETS_BLK)
        edge = dot_nn(edge_pin[of, :], table[cells:, :])
        taken[of, :] = (edge + local_taken[of, :].astype(F32)).astype(BF16)
        net_sum = dot_nn(pin_net[:, of], taken[of, :feat])
        net_feats[nets_of, :] = (net_sum * net_inverse(pin_net[:, of])).astype(BF16)
    net_pre = dot_nn(net_feats[...], w_net_ref[...]).astype(BF16)
    scale = 0.7978845608028654
    for b in range(blocks):
        of = slice(b * pins, (b + 1) * pins)
        nets_of = slice(b * NETS_BLK, (b + 1) * NETS_BLK)
        pre = dot_nn(taken[of, :feat], w_in_ref[...]) + dot_nn(net_pin[of, :], net_pre[nets_of]) + bias_ref[...]
        pulled = dot_nt(taken[of, feat:], w_out_ref[...])
        square = pre * pre
        bend = jnp.tanh(pre * (scale + (scale * 0.044715) * square))
        half = 0.5 * bend + 0.5
        terms[of, :hid] = (pre * half).astype(BF16)
        slope = half + (0.5 * pre) * (1.0 - bend * bend) * (scale + (3 * scale * 0.044715) * square)
        pre_grad = (pulled * slope).astype(BF16)
        terms[of, hid:] = pre_grad
        net_grads[nets_of, :] = dot_nn(pin_net[:, of], pre_grad).astype(BF16)
    sums[...] = dot_nn(at_row[...], terms[...])
    outgoing = start_copies([(sums, sums_hbm), (net_grads, net_grads_hbm)], out_sems)
    hidden_high, hidden_low = split_bf16(sums[:, :hid])
    grad_high, grad_low = split_bf16(sums[:, hid:])
    for copy in copies:
        copy.wait()
    table_x, table_g = table[:, :feat], table[:, feat:]
    acc_in = dot_tn(table_x, grad_high) + dot_tn(table_x, grad_low)
    acc_out = dot_tn(hidden_high, table_g) + dot_tn(hidden_low, table_g)
    acc_net = dot_tn(net_feats[...], net_grads[...])
    acc_bias = jnp.broadcast_to(jnp.sum(sums[:, hid:], axis=0, keepdims=True), (8, hid))
    if fast:
        part_count, rows, _ = grads_ref.shape
        part = feat // part_count
        for to in range(part_count):
            of = slice(to * part, (to + 1) * part)
            blocks_of = [acc_in[of, :], acc_net[of, :], acc_out[of, :], acc_bias]
            grads_ref[to] = jnp.concatenate([x.astype(BF16) for x in blocks_of], axis=0)
    else:
        grads_ref[:feat, :] = acc_in
        grads_ref[feat : 2 * feat, :] = acc_net
        grads_ref[2 * feat : 2 * feat + hid, :] = acc_out
        grads_ref[2 * feat + hid :, :] = acc_bias
    for copy in outgoing:
        copy.wait()


def back_kernel(fast, pos_ref, ids_hbm, sums_hbm, net_grads_hbm, w_in_hbm, w_net_hbm, w_out_hbm, *rest):
    *outs, ids, wide, sums, net_grads, w_in_ref, w_net_ref, w_out_ref, sems, at_row, net_backs, acc = rest
    table_len = acc.shape[0]
    feat, hid = w_in_ref.shape
    blocks = net_grads.shape[0] // NETS_BLK
    pins = ids.shape[1]
    mine = pl.ds(pl.multiple_of(pos_ref[1] * hid, hid), hid)
    copies = start_copies(
        [
            (ids_hbm, ids),
            (net_grads_hbm, net_grads),
            (w_net_hbm.at[:, mine], w_net_ref),
            (w_in_hbm.at[:, mine], w_in_ref),
            (w_out_hbm.at[mine, :], w_out_ref),
            (sums_hbm, sums),
        ],
        sems,
    )
    copies[0].wait()
    columns = id_columns(ids, wide)
    rows = ids[...].astype(jnp.int32)
    for b in range(blocks):
        of = slice(b * pins, (b + 1) * pins)
        for t, tile in enumerate(tiled_rows(rows[8 + b : 9 + b, :], table_len)):
            at_row[t * 128 : (t + 1) * 128, of] = tile
    for copy in copies[1:3]:
        copy.wait()
    for b in range(blocks):
        of = slice(b * pins, (b + 1) * pins)
        nets_of = slice(b * NETS_BLK, (b + 1) * NETS_BLK)
        inverse = net_inverse(row_onehot(NETS_BLK, rows[b : b + 1, :]))
        feat_grad = (dot_nt(net_grads[nets_of, :], w_net_ref[...]) * inverse).astype(BF16)
        net_backs[of, :] = dot_nn(column_onehot(columns[:, b : b + 1], NETS_BLK), feat_grad).astype(BF16)
    for copy in copies[3:]:
        copy.wait()
    hidden_high, hidden_low = split_bf16(sums[:, :hid])
    grad_high, grad_low = split_bf16(sums[:, hid:])
    acc[:, :feat] = dot_nn(hidden_high, w_out_ref[...]) + dot_nn(hidden_low, w_out_ref[...])
    acc[:, feat:] = (
        dot_nt(grad_high, w_in_ref[...]) + dot_nt(grad_low, w_in_ref[...]) + dot_nn(at_row[...], net_backs[...])
    )
    if fast:
        own_ref, far_ref, twin_ref = outs
        length = own_ref.shape[0]
        cells = table_len - 128
        share = cells // 4
        edges = acc[cells:, :].astype(BF16)
        row = lax.broadcasted_iota(jnp.int32, (length - share, 128), 0)
        lane = lax.broadcasted_iota(jnp.int32, row.shape, 1)
        for bits, ref, at in ((0, own_ref, 0), (2, far_ref, 0), (1, twin_ref, 0), (3, twin_ref, length)):
            to = pos_ref[1] ^ bits
            rows = acc[pl.ds(pl.multiple_of(to * share, share), share), :]
            ref[at : at + share, :] = rows.astype(ref.dtype)
            of = lane == ((row >> 2) * 16 + to * 4 + (row & 3))
            ref[at + share : at + length, :] = dot_nn(of.astype(BF16), edges).astype(ref.dtype)
        return
    own_ref, send_ref = outs
    cells = own_ref.shape[0]
    own_ref[...] = acc[:cells, :]
    part_count, rows, _ = send_ref.shape
    slots = rows // 2
    for part in range(part_count):
        of = slice(cells + part * slots, cells + (part + 1) * slots)
        send_ref[part, :slots, :] = acc[of, :feat].astype(BF16)
        send_ref[part, slots:, :] = acc[of, feat:].astype(BF16)


def pair_kernel(own_ref, far_ref, twin_ref, own_sum_ref, far_sum_ref):
    length = own_ref.shape[0]
    own_sum_ref[...] = own_ref[...] + twin_ref[:length, :].astype(F32)
    far_sum_ref[...] = (far_ref[...] + twin_ref[length:, :].astype(F32)).astype(BF16)


def sum_kernel(got_ref, own_ref, *rest):
    far_ref, *payloads, rows_ref, bias_ref = rest
    total = own_ref[...] + far_ref[...].astype(F32)
    share, wide = rows_ref.shape
    feat = wide // 2
    rows_ref[...] = total[:share]
    piece = got_ref[0].astype(F32)
    for part in range(1, got_ref.shape[0]):
        piece += got_ref[part].astype(F32)
    rows = piece.shape[0] - 8
    bias_ref[...] = jnp.concatenate([piece[rows:]] * 2, axis=0).astype(BF16)
    for k, payload in enumerate(payloads):
        edges = []
        for odd in range(2):
            at = share + 4 * (2 * k + odd)
            edges += [total[at : at + 4, :feat], total[at : at + 4, feat:]]
        payload[...] = jnp.concatenate([piece[:rows]] + edges, axis=0).astype(BF16)


def place(pos_ref, parts, outs, buffer, sems):
    rows, hid = buffer.shape[1:]
    part = rows // 3
    copies = []
    for at, (ref, start, cell_bits, net_bits) in enumerate(parts):
        row = pl.multiple_of((pos_ref[0] ^ cell_bits) * part, part)
        first = pl.multiple_of((pos_ref[1] ^ net_bits) * hid, hid)
        buffer[at] = ref[start : start + rows, :].astype(F32)
        targets = [
            outs[0].at[pl.ds(row, part), pl.ds(first, hid)],
            outs[1].at[pl.ds(row, part), pl.ds(first, hid)],
            outs[2].at[pl.ds(pl.multiple_of(first + row, part), part), :],
        ]
        for matrix, target in enumerate(targets):
            source = buffer.at[at, matrix * part : (matrix + 1) * part, :]
            copies.append(pltpu.make_async_copy(source, target, sems.at[3 * at + matrix]))
            copies[-1].start()
    return copies


def place_kernel(tags, olds, pos_ref, *refs):
    ins, refs = refs[: len(tags)], refs[len(tags) + olds :]
    outs, (buffer, sems) = refs[:3], refs[3:]
    parts = [(ref,) + tag for ref, some in zip(ins, tags) for tag in some]
    for copy in place(pos_ref, parts, outs, buffer, sems):
        copy.wait()


def edge_rows(edges):
    return jnp.concatenate([edge[:64, :] for edge in edges], axis=0)


def first_kernel(tags, pos_ref, idx_ref, x_hbm, g_hbm, rows_ref, *refs):
    ins, refs = refs[: len(tags)], refs[len(tags) :]
    edges, refs = refs[:2], refs[2:]
    grads, (total_ref, pick_y_ref, pick_x_ref, buffer, sems, x_ref, g_ref, row_sems) = refs[:3], refs[3:]
    share, wide = rows_ref.shape
    feat = wide // 2
    cell, net = pos_ref[0], pos_ref[1]
    mine = pl.ds(pl.multiple_of(net * share, share), share)
    copies = start_copies([(x_hbm.at[mine, :], x_ref), (g_hbm.at[mine, :], g_ref)], row_sems)
    parts = [(ref,) + tag for ref, some in zip(ins, tags) for tag in some]
    placed = place(pos_ref, parts, grads, buffer, sems)
    lane = lax.broadcasted_iota(jnp.int32, (1, 256), 1)
    bits, source, is_back, slot = lane >> 6, (lane >> 3) & 7, (lane >> 2) & 1, lane & 3
    part_of = cell ^ (((source & 3) << 1) | (source >> 2))
    ids = pick_ids(idx_ref[0], part_of, ((net ^ bits) << 2) | slot) - net * share
    pick_y = row_onehot(share, jnp.where(is_back == 0, ids, -1))
    pick_x = row_onehot(share, jnp.where(is_back == 1, ids, -1))
    pick_y_ref[...] = pick_y[:, 128:]
    pick_x_ref[...] = pick_x[:, 128:]
    halo = edge_rows(edges)
    for copy in copies:
        copy.wait()
    total_ref[:, :feat] = x_ref[...].astype(F32) + rows_ref[:, :feat] + dot_nn(pick_y[:, :128], halo)
    total_ref[:, feat:] = g_ref[...].astype(F32) + rows_ref[:, feat:] + dot_nn(pick_x[:, :128], halo)
    for copy in placed:
        copy.wait()


def finish_kernel(tags, pos_ref, total_ref, pick_y_ref, pick_x_ref, *refs):
    ins, refs = refs[: len(tags)], refs[len(tags) :]
    edges, refs = refs[:4], refs[4 + 3 :]
    grads, (updated_ref, back_ref, bias_ref, buffer, sems) = refs[:3], refs[3:]
    feat = updated_ref.shape[1]
    parts = [(ref,) + tag for ref, some in zip(ins, tags) for tag in some]
    placed = place(pos_ref, parts, grads, buffer, sems)
    halo = edge_rows(edges[2:])
    updated_ref[...] = (total_ref[:, :feat] + dot_nn(pick_y_ref[...], halo)).astype(BF16)
    back_ref[...] = (total_ref[:, feat:] + dot_nn(pick_x_ref[...], halo)).astype(BF16)
    for bits, edge in enumerate(edges):
        at = pl.multiple_of((pos_ref[1] ^ bits) * feat, feat)
        bias_ref[:, pl.ds(at, feat)] = edge[64:, :].astype(F32)[:1]
    for copy in placed:
        copy.wait()


def combine_kernel(pos_ref, idx_ref, got_ref, own_ref, *outs):
    part_count, slots = idx_ref.shape[1:]
    cells, wide = own_ref.shape
    feat = wide // 2
    group = 128 // slots
    rows_y = own_ref[:, :feat]
    rows_x = own_ref[:, feat:]
    for first in range(0, part_count, group):
        onehot = slot_onehot(idx_ref[0, first : first + group], cells)
        y = got_ref[first : first + group, :slots, :].reshape(128, feat)
        x = got_ref[first : first + group, slots:, :].reshape(128, feat)
        rows_y += dot_nn(onehot, y)
        rows_x += dot_nn(onehot, x)
    *shares, scratch = outs
    scratch[:, :feat] = rows_y
    scratch[:, feat:] = rows_x
    share = cells // len(shares)
    for bits, share_ref in enumerate(shares):
        at = pl.multiple_of((pos_ref[1] ^ bits) * share, share)
        share_ref[...] = scratch[pl.ds(at, share), :].astype(share_ref.dtype)


def plain_rows_kernel(pos_ref, x_hbm, g_hbm, own_ref, *rest):
    *others, updated_ref, back_ref, x_ref, g_ref, sems = rest
    share, feat = updated_ref.shape
    mine = pl.ds(pl.multiple_of(pos_ref[1] * share, share), share)
    copies = start_copies([(x_hbm.at[mine, :], x_ref), (g_hbm.at[mine, :], g_ref)], sems)
    total = own_ref[...]
    for other in others:
        total += other[...].astype(F32)
    for copy in copies:
        copy.wait()
    updated_ref[...] = (x_ref[...].astype(F32) + total[:, :feat]).astype(BF16)
    back_ref[...] = (g_ref[...].astype(F32) + total[:, feat:]).astype(BF16)


def whole(count):
    return [pl.BlockSpec(memory_space=pltpu.VMEM)] * count


SMEM = pl.BlockSpec(memory_space=pltpu.SMEM)
HBM = pl.BlockSpec(memory_space=pltpu.HBM)
PARAMS = dict(compiler_params=pltpu.CompilerParams(vmem_limit_bytes=VMEM_LIMIT))


def about(microseconds):
    return pl.CostEstimate(flops=0, transcendentals=0, bytes_accessed=int(microseconds * 3.6e6))


def in_hbm(*arrays):
    return [pltpu.with_memory_space_constraint(x, pltpu.HBM) for x in arrays]


def flip(x, axis, bits):
    size = lax.axis_size(axis)
    return lax.ppermute(x, axis, [(i, i ^ bits) for i in range(size)])


def both(x, cell_bits, net_bits):
    parts, group = lax.axis_size("cell"), lax.axis_size("net")
    pairs = [
        (c * group + n, (c ^ cell_bits(n)) * group + (n ^ net_bits)) for c in range(parts) for n in range(group)
    ]
    return lax.ppermute(x, ("cell", "net"), pairs)


def local(cell_feat, out_grad, w_in, w_net, bias, w_out, send_idx, pin_net, pin_ref, block_count):
    part_count = lax.axis_size("cell")
    group_size = lax.axis_size("net")
    cells, feat = cell_feat.shape
    hidden_dim = w_in.shape[1]
    hid = hidden_dim // group_size
    slots = send_idx.shape[2]
    pins = pin_net.shape[3]
    table_len = cells + part_count * slots
    fast = part_count == 8 and group_size == 4
    pos = jnp.stack([lax.axis_index("cell"), lax.axis_index("net")]).astype(jnp.int32)

    def shape(dtype, *dims):
        return jax.ShapeDtypeStruct(dims, dtype)

    if fast:
        sent_shape = [shape(BF16, 2, slots, 2 * feat)] * 4
    else:
        sent_shape = [shape(BF16, part_count, slots, 2 * feat)]
    ints, *sent = pl.pallas_call(
        functools.partial(gather_kernel, fast),
        in_specs=whole(1) + [HBM] * 5,
        out_specs=whole(1 + len(sent_shape)),
        out_shape=[shape(jnp.int32, 1, 8, pins)] + sent_shape,
        scratch_shapes=[
            pltpu.VMEM(send_idx.shape, jnp.int32),
            pltpu.VMEM((cells, feat), BF16),
            pltpu.VMEM((cells, feat), BF16),
            pltpu.VMEM(pin_net.shape, jnp.int32),
            pltpu.VMEM(pin_ref.shape, jnp.int32),
            pltpu.SemaphoreType.DMA((5,)),
        ],
        name="take_boundary",
        cost_estimate=about(2.0),
        **PARAMS,
    )(block_count, *in_hbm(send_idx, cell_feat, out_grad, pin_net, pin_ref))
    if fast:
        all_ints = jnp.concatenate([ints, flip(ints, "net", 1)])
        all_ints = [all_ints, flip(all_ints, "net", 2)]
        near = [sent[0]] + [flip(sent[k], "cell", 2 * k) for k in (1, 2, 3)]
        cross = jnp.stack([a[1] for a in near])
    else:
        halo = [lax.all_to_all(sent[0], "cell", split_axis=0, concat_axis=0, tiled=True)]
        all_ints = [lax.all_gather(ints, "net", tiled=True)]

    blocks = group_size + 1
    part = feat // part_count
    share = cells // group_size
    edge = part_count * slots // group_size
    all_pins = blocks * pins
    spread_shape = [
        shape(BF16, all_pins, cells),
        shape(BF16, table_len, all_pins),
        shape(BF16, all_pins, NETS_BLK),
        shape(BF16, NETS_BLK, all_pins),
        shape(BF16, all_pins, table_len - cells),
        shape(BF16, feat, hid),
        shape(BF16, feat, hid),
        shape(F32, 1, hid),
        shape(BF16, hid, feat),
    ]
    ids, at_pin, *spread = pl.pallas_call(
        functools.partial(spread_kernel, fast, slots),
        in_specs=[SMEM] + whole(len(all_ints)) + [HBM] * 4,
        out_specs=[HBM] + whole(9),
        out_shape=[pltpu.HBM((16, pins), F32)] + spread_shape,
        scratch_shapes=[
            pltpu.VMEM((16, pins), F32),
            pltpu.VMEM((128, pins), F32),
            pltpu.SemaphoreType.DMA((4,)),
            pltpu.SemaphoreType.DMA,
        ],
        name="spread",
        cost_estimate=about(4.5),
        **PARAMS,
    )(pos, *all_ints, *in_hbm(w_in, w_net, bias.reshape(1, hidden_dim), w_out))
    if fast:
        cross, at_pin = lax.optimization_barrier((cross, at_pin))
        halo = near + [flip(cross, "cell", 1)]
    taken = pl.pallas_call(
        own_pins_kernel,
        in_specs=[pl.BlockSpec(memory_space=pl.ANY)] + whole(1) + [HBM] * 2,
        out_specs=whole(1)[0],
        out_shape=shape(BF16, all_pins, 2 * feat),
        scratch_shapes=[pltpu.VMEM((cells, 2 * feat), BF16), pltpu.SemaphoreType.DMA((2,))],
        name="own_pins",
        cost_estimate=about(2.5),
        **PARAMS,
    )(cross if fast else halo[0], at_pin, *in_hbm(cell_feat, out_grad))

    grads, sums, net_grads = pl.pallas_call(
        functools.partial(layer_kernel, fast, len(halo)),
        in_specs=whole(len(halo) + 9) + [HBM] * 2,
        out_specs=whole(1) + [HBM] * 2,
        out_shape=[
            shape(BF16, part_count, 3 * part + 8, feat) if fast else shape(F32, 2 * feat + hid + 8, hid),
            pltpu.HBM((table_len, 2 * hid), F32),
            pltpu.HBM((blocks * NETS_BLK, hid), BF16),
        ],
        scratch_shapes=[
            pltpu.VMEM((table_len, 2 * feat), BF16),
            pltpu.SemaphoreType.DMA((2,)),
            pltpu.VMEM((table_len, 2 * hid), F32),
            pltpu.VMEM((blocks * NETS_BLK, hid), BF16),
            pltpu.SemaphoreType.DMA((2,)),
            pltpu.VMEM((all_pins, 2 * feat), BF16),
            pltpu.VMEM((blocks * NETS_BLK, feat), BF16),
            pltpu.VMEM((all_pins, 2 * hid), BF16),
        ],
        name="layer",
        cost_estimate=about(7.7),
        **PARAMS,
    )(*halo, *spread, taken, *in_hbm(cell_feat, out_grad))

    if fast:
        got = lax.all_to_all(grads, "cell", split_axis=0, concat_axis=0, tiled=True)
        length = share + edge
        out_shape = [shape(F32, length, 2 * feat)] * 2 + [shape(BF16, 2 * length, 2 * feat)]
    else:
        out_shape = [shape(F32, cells, 2 * feat), shape(BF16, part_count, 2 * slots, feat)]
    outs = pl.pallas_call(
        functools.partial(back_kernel, fast),
        in_specs=[SMEM] + [HBM] * 6,
        out_specs=whole(len(out_shape)),
        out_shape=out_shape,
        scratch_shapes=[
            pltpu.VMEM((16, pins), F32),
            pltpu.VMEM((128, pins), F32),
            pltpu.VMEM((table_len, 2 * hid), F32),
            pltpu.VMEM((blocks * NETS_BLK, hid), BF16),
            pltpu.VMEM((feat, hid), BF16),
            pltpu.VMEM((feat, hid), BF16),
            pltpu.VMEM((hid, feat), BF16),
            pltpu.SemaphoreType.DMA((6,)),
            pltpu.VMEM((table_len, blocks * pins), BF16),
            pltpu.VMEM((blocks * pins, feat), BF16),
            pltpu.VMEM((table_len, 2 * feat), F32),
        ],
        name="back",
        cost_estimate=about(4.6),
        **PARAMS,
    )(pos, *in_hbm(ids, sums, net_grads, w_in, w_net, w_out))

    row_shapes = [shape(BF16, share, feat)] * 2
    row_scratch = [
        pltpu.VMEM((share, feat), BF16),
        pltpu.VMEM((share, feat), BF16),
        pltpu.SemaphoreType.DMA((2,)),
    ]
    grad_shapes = [shape(F32, feat, hidden_dim), shape(F32, feat, hidden_dim), shape(F32, hidden_dim, feat)]
    if not fast:
        own, send = outs
        got = lax.all_to_all(send, "cell", split_axis=0, concat_axis=0, tiled=True)
        shares = pl.pallas_call(
            combine_kernel,
            in_specs=[SMEM] + whole(3),
            out_specs=whole(group_size),
            out_shape=[shape(BF16 if bits else F32, share, 2 * feat) for bits in range(group_size)],
            scratch_shapes=[pltpu.VMEM((cells, 2 * feat), F32)],
            name="combine",
            **PARAMS,
        )(pos, send_idx, got, own)
        others = [flip(shares[bits], "net", bits) for bits in range(1, group_size)]
        updated, cell_grad = pl.pallas_call(
            plain_rows_kernel,
            in_specs=[SMEM] + [HBM] * 2 + whole(group_size),
            out_specs=whole(2),
            out_shape=row_shapes,
            scratch_shapes=row_scratch,
            name="own_rows",
            **PARAMS,
        )(pos, *in_hbm(cell_feat, out_grad), shares[0], *others)
        summed = lax.all_gather(lax.psum(grads, "cell"), "net")
        grad_in = jnp.moveaxis(summed[:, :feat], 0, 1).reshape(feat, hidden_dim)
        grad_net = jnp.moveaxis(summed[:, feat : 2 * feat], 0, 1).reshape(feat, hidden_dim)
        grad_out = summed[:, 2 * feat : 2 * feat + hid].reshape(hidden_dim, feat)
        grad_bias = summed[:, 2 * feat + hid].reshape(hidden_dim)
        return (updated, cell_grad, grad_in, grad_net, grad_bias, grad_out)

    own, far, twin_share = outs
    own, far = pl.pallas_call(
        pair_kernel,
        in_specs=whole(3),
        out_specs=whole(2),
        out_shape=[shape(F32, length, 2 * feat), shape(BF16, length, 2 * feat)],
        name="pairs",
        **PARAMS,
    )(own, far, flip(twin_share, "net", 1))
    rows_of = 3 * part
    *pays, rows, bias_sum = pl.pallas_call(
        sum_kernel,
        in_specs=whole(3),
        out_specs=whole(6),
        out_shape=[shape(BF16, rows_of + 16, feat)] * 4 + [shape(F32, share, 2 * feat), shape(BF16, 16, feat)],
        name="sums",
        cost_estimate=about(0.2),
        **PARAMS,
    )(got, own, flip(far, "net", 2))
    near = [pays[0]] + [flip(pays[k], "cell", 2 * k) for k in (1, 2, 3)]
    across = flip(jnp.concatenate(near[:2] + [a[rows_of:] for a in near[2:]]), "cell", 1)
    second = jnp.concatenate([a[:rows_of] for a in near[2:]])
    second = jnp.concatenate([second, flip(second, "net", 2)])
    starts = [rows_of, 2 * rows_of + 16, 2 * rows_of + 32, 2 * rows_of + 48]
    edges = [a[rows_of : rows_of + 8] for a in near] + [across[at + 8 : at + 16] for at in starts]
    full = rows_of + 16
    pieces = [near[0][:rows_of], near[1][:rows_of], across[:rows_of], across[full : full + rows_of]]
    first = jnp.concatenate(pieces + edges + [bias_sum])
    early = [flip(first, "net", 1), flip(second, "net", 1)]
    third, fourth = flip(first, "net", 2), flip(second, "cell", 1)
    first_tag = [(0, 0, 0), (rows_of, 2, 0), (2 * rows_of, 1, 0), (3 * rows_of, 3, 0)]
    second_tag = [(0, 4, 0), (rows_of, 6, 0), (2 * rows_of, 4, 2), (3 * rows_of, 6, 2)]
    early_tags = [first_tag, second_tag]
    late_tags = [[(at, c, n ^ 2) for at, c, n in first_tag], [(at, c ^ 1, n) for at, c, n in second_tag]]

    def twin(tags):
        return [[(at, c, n ^ 1) for at, c, n in tag] for tag in tags]

    def scratch(arrays):
        return [pltpu.VMEM((4 * len(arrays), rows_of, hid), F32), pltpu.SemaphoreType.DMA((12 * len(arrays),))]

    *grads, total, pick_y, pick_x = pl.pallas_call(
        functools.partial(first_kernel, early_tags + twin(early_tags)),
        in_specs=[SMEM] + whole(1) + [HBM] * 2 + whole(1 + 4 + 2),
        out_specs=[HBM] * 3 + whole(3),
        out_shape=grad_shapes + [shape(F32, share, 2 * feat)] + [shape(BF16, share, 128)] * 2,
        scratch_shapes=scratch([0] * 4) + row_scratch,
        name="first_pieces",
        **PARAMS,
    )(pos, send_idx, *in_hbm(cell_feat, out_grad), rows, first, second, *early, first[4 * rows_of :], early[0][4 * rows_of :])
    third, fourth, grads = lax.optimization_barrier((third, fourth, grads))
    late = [flip(third, "net", 1), flip(fourth, "net", 1)]
    grads = pl.pallas_call(
        functools.partial(place_kernel, late_tags, 3),
        in_specs=[SMEM] + whole(2) + [HBM] * 3,
        out_specs=[HBM] * 3,
        out_shape=grad_shapes,
        scratch_shapes=scratch(late),
        input_output_aliases={3 + i: i for i in range(3)},
        name="place",
        **PARAMS,
    )(pos, third, fourth, *grads)
    all_edges = [a[4 * rows_of :] for a in (first, early[0], third, late[0])]
    grad_in, grad_net, grad_out, updated, cell_grad, grad_bias = pl.pallas_call(
        functools.partial(finish_kernel, twin(late_tags)),
        in_specs=[SMEM] + whole(3 + 2 + 4) + [HBM] * 3,
        out_specs=[HBM] * 3 + whole(3),
        out_shape=grad_shapes + row_shapes + [shape(F32, 1, hidden_dim)],
        scratch_shapes=scratch(late),
        input_output_aliases={4 + 2 + 4 + i: i for i in range(3)},
        name="finish",
        **PARAMS,
    )(pos, total, pick_y, pick_x, *late, *all_edges, *grads)
    return (updated, cell_grad, grad_in, grad_net, grad_bias.reshape(hidden_dim), grad_out)


def solution(mesh):
    placed = (
        P("cell", None),
        P("cell", None),
        P(),
        P(),
        P(),
        P(),
        P("cell", None, None),
        P("cell", "net", None, None),
        P("cell", "net", None, None),
        P("cell", "net"),
    )
    return jax.shard_map(
        local,
        mesh=mesh,
        in_specs=placed,
        out_specs=(P(("cell", "net"), None), P(("cell", "net"), None), P(), P(), P(), P()),
        check_vma=False,
    )
```

```python
import functools

import jax
import jax.numpy as jnp
from jax import lax
from jax.experimental import pallas as pl
from jax.experimental.pallas import tpu as pltpu
from jax.sharding import PartitionSpec as P

NETS_BLK = 128
BF16 = jnp.bfloat16
F32 = jnp.float32
VMEM_LIMIT = 40 * 1024 * 1024


def dot_nn(a, b):
    return jnp.dot(a, b, preferred_element_type=F32)


def dot_nt(a, b):
    return lax.dot_general(a, b, (((1,), (1,)), ((), ())), preferred_element_type=F32)


def dot_tn(a, b):
    return lax.dot_general(a, b, (((0,), (0,)), ((), ())), preferred_element_type=F32)


def pick_ids(idx, part_of, slot_of):
    parts, slots = idx.shape
    lanes = part_of.shape[1]
    spread = (lax.broadcasted_iota(jnp.int32, (slots, lanes), 0) == slot_of).astype(BF16)
    high = dot_nn((idx >> 6).astype(F32).astype(BF16), spread)
    low = dot_nn((idx & 63).astype(F32).astype(BF16), spread)
    mine = lax.broadcasted_iota(jnp.int32, (parts, lanes), 0) == part_of
    return jnp.sum(jnp.where(mine, high * 64.0 + low, 0.0), axis=0, keepdims=True).astype(jnp.int32)


def slot_onehot(idx, cells):
    parts, slots = idx.shape
    lane = lax.broadcasted_iota(jnp.int32, (1, parts * slots), 1)
    return row_onehot(cells, pick_ids(idx, lane // slots, lane % slots))


def start_copies(pairs, sems):
    copies = [pltpu.make_async_copy(src, dst, sems.at[i]) for i, (src, dst) in enumerate(pairs)]
    for copy in copies:
        copy.start()
    return copies


def gather_kernel(fast, count_ref, idx_hbm, x_hbm, g_hbm, net_hbm, ref_hbm, ints_ref, *rest):
    *outs, idx_ref, x_ref, g_ref, net_ref, ref_ref, sems = rest
    copies = start_copies(
        [(idx_hbm, idx_ref), (x_hbm, x_ref), (g_hbm, g_ref), (net_hbm, net_ref), (ref_hbm, ref_ref)], sems
    )
    for copy in copies:
        copy.wait()
    slot_max = net_ref.shape[2]
    ints_ref[0] = jnp.broadcast_to(count_ref[...], ints_ref.shape[1:])
    ints_ref[0, :slot_max, :] = net_ref[0, 0]
    ints_ref[0, slot_max : 2 * slot_max, :] = ref_ref[0, 0]
    part_count, slots = idx_ref.shape[1:]
    cells, feat = x_ref.shape
    if fast:
        cell = lax.axis_index("cell")
        order = [cell ^ bits for bits in range(part_count)]
        idx = jnp.concatenate([idx_ref[0, pl.ds(part, 1), :] for part in order], axis=0)
        onehot = slot_onehot(idx, cells)
        for at, values in ((0, x_ref), (feat, g_ref)):
            rows = dot_tn(onehot, values[...]).astype(BF16)
            for k, out_ref in enumerate(outs):
                out_ref[:, :, at : at + feat] = rows[32 * k : 32 * (k + 1)].reshape(2, slots, feat)
        return
    (out_ref,) = outs
    group = 128 // slots
    for first in range(0, part_count, group):
        onehot = slot_onehot(idx_ref[0, first : first + group], cells)
        for at, values in ((0, x_ref), (feat, g_ref)):
            rows = dot_tn(onehot, values[...]).astype(BF16)
            out_ref[first : first + group, :, at : at + feat] = rows.reshape(group, slots, feat)


def split_bf16(x):
    high = x.astype(BF16)
    return high, (x - high.astype(F32)).astype(BF16)


def block_ids(ints_refs):
    nets, refs = [], []
    pins = ints_refs[0].shape[2]
    extra_net = jnp.zeros((1, pins), jnp.int32)
    extra_ref = jnp.zeros((1, pins), jnp.int32)
    for ints in [ref[i] for ref in ints_refs for i in range(ref.shape[0])]:
        nets.append(ints[0:1, :])
        refs.append(ints[2:3, :])
        second = ints[4:5, :] > 1
        extra_net += jnp.where(second, ints[1:2, :] + 1, 0)
        extra_ref += jnp.where(second, ints[3:4, :] + 1, 0)
    nets.append(extra_net - 1)
    refs.append(extra_ref - 1)
    return nets, refs


def row_onehot(rows, ids):
    return (lax.broadcasted_iota(jnp.int32, (rows, ids.shape[1]), 0) == ids).astype(BF16)


def column_onehot(ids, lanes):
    return (lax.broadcasted_iota(jnp.int32, (ids.shape[0], lanes), 1) == ids).astype(BF16)


def tiled_columns(ids, length):
    low = column_onehot(ids & 127, 128)
    high = jnp.broadcast_to((ids >> 7).astype(F32).astype(BF16), low.shape)
    return [jnp.where(high == t, low, jnp.zeros((), BF16)) for t in range(length // 128)]


def tiled_rows(ids, length):
    low = row_onehot(128, ids & 127)
    high = jnp.broadcast_to((ids >> 7).astype(F32).astype(BF16), low.shape)
    return [jnp.where(high == t, low, jnp.zeros((), BF16)) for t in range(length // 128)]


def net_inverse(pin_net):
    return 1.0 / jnp.maximum(jnp.sum(pin_net.astype(F32), axis=1, keepdims=True), 1.0)


def id_columns(ids, wide):
    wide[...] = jnp.zeros_like(wide)
    wide[:16, :] = ids[...]
    return wide[...].T.astype(jnp.int32)


def spread_kernel(fast, slots, pos_ref, *refs):
    ints_refs, refs = refs[:-18], refs[-18:]
    w_in_hbm, w_net_hbm, bias_hbm, w_out_hbm, ids_hbm, *refs = refs
    at_pin, at_row, net_pin, pin_net, edge_pin, w_in_ref, w_net_ref, bias_ref, w_out_ref, *refs = refs
    ids, wide, sems, out_sem = refs
    cells = at_pin.shape[1]
    hid = w_in_ref.shape[1]
    pins = ids.shape[1]
    table_len = at_row.shape[0]
    mine = pl.ds(pl.multiple_of(pos_ref[1] * hid, hid), hid)
    copies = start_copies(
        [
            (w_in_hbm.at[:, mine], w_in_ref),
            (w_net_hbm.at[:, mine], w_net_ref),
            (bias_hbm.at[:, mine], bias_ref),
            (w_out_hbm.at[mine, :], w_out_ref),
        ],
        sems,
    )
    nets, refs = block_ids(ints_refs)
    blocks = len(nets)
    if fast:
        refs = [jnp.where(row < cells, row, ((row - cells) ^ (pos_ref[0] * slots)) + cells) for row in refs]
    ids[...] = jnp.zeros_like(ids)
    for b in range(blocks):
        ids[b : b + 1, :] = nets[b].astype(F32)
        ids[8 + b : 9 + b, :] = refs[b].astype(F32)
    outgoing = pltpu.make_async_copy(ids, ids_hbm, out_sem)
    outgoing.start()
    columns = id_columns(ids, wide)
    for b in range(blocks):
        of = slice(b * pins, (b + 1) * pins)
        as_columns, as_rows = tiled_columns(columns[:, 8 + b : 9 + b], table_len), tiled_rows(refs[b], table_len)
        for t, (tile_column, tile_row) in enumerate(zip(as_columns, as_rows)):
            if t < cells // 128:
                at_pin[of, t * 128 : (t + 1) * 128] = tile_column
            else:
                edge_pin[of, t * 128 - cells : (t + 1) * 128 - cells] = tile_column
            at_row[t * 128 : (t + 1) * 128, of] = tile_row
        net_pin[of, :] = column_onehot(columns[:, b : b + 1], NETS_BLK)
        pin_net[:, of] = row_onehot(NETS_BLK, nets[b])
    for copy in copies:
        copy.wait()
    outgoing.wait()


def own_pins_kernel(after_ref, at_pin, x_hbm, g_hbm, taken, table, sems):
    feat = x_hbm.shape[1]
    copies = start_copies([(x_hbm, table.at[:, :feat]), (g_hbm, table.at[:, feat:])], sems)
    for copy in copies:
        copy.wait()
    taken[...] = dot_nn(at_pin[...], table[...]).astype(BF16)


def layer_kernel(fast, halos, *refs):
    halo_refs, refs = refs[:halos], refs[halos:]
    at_row, net_pin, pin_net, edge_pin, w_in_ref, w_net_ref, bias_ref, w_out_ref, local_taken, *refs = refs
    x_hbm, g_hbm, grads_ref, sums_hbm, net_grads_hbm, *refs = refs
    table, sems, sums, net_grads, out_sems, taken, net_feats, terms = refs
    cells, feat = x_hbm.shape
    hid = w_in_ref.shape[1]
    table_len, pin_count = at_row.shape
    blocks = net_grads.shape[0] // NETS_BLK
    pins = pin_count // blocks
    copies = start_copies([(x_hbm, table.at[:cells, :feat]), (g_hbm, table.at[:cells, feat:])], sems)
    if fast:
        *near, cross = halo_refs
        blocks_of = [block for k, ref in enumerate(near) for block in (ref[0], cross[k])]
        table[cells:, :] = jnp.concatenate(blocks_of, axis=0)
    else:
        table[cells:, :] = halo_refs[0][...].reshape(table_len - cells, 2 * feat)
    for b in range(blocks):
        of = slice(b * pins, (b + 1) * pins)
        nets_of = slice(b * NETS_BLK, (b + 1) * NETS_BLK)
        edge = dot_nn(edge_pin[of, :], table[cells:, :])
        taken[of, :] = (edge + local_taken[of, :].astype(F32)).astype(BF16)
        net_sum = dot_nn(pin_net[:, of], taken[of, :feat])
        net_feats[nets_of, :] = (net_sum * net_inverse(pin_net[:, of])).astype(BF16)
    net_pre = dot_nn(net_feats[...], w_net_ref[...]).astype(BF16)
    scale = 0.7978845608028654
    for b in range(blocks):
        of = slice(b * pins, (b + 1) * pins)
        nets_of = slice(b * NETS_BLK, (b + 1) * NETS_BLK)
        pre = dot_nn(taken[of, :feat], w_in_ref[...]) + dot_nn(net_pin[of, :], net_pre[nets_of]) + bias_ref[...]
        pulled = dot_nt(taken[of, feat:], w_out_ref[...])
        square = pre * pre
        bend = jnp.tanh(pre * (scale + (scale * 0.044715) * square))
        half = 0.5 * bend + 0.5
        terms[of, :hid] = (pre * half).astype(BF16)
        slope = half + (0.5 * pre) * (1.0 - bend * bend) * (scale + (3 * scale * 0.044715) * square)
        pre_grad = (pulled * slope).astype(BF16)
        terms[of, hid:] = pre_grad
        net_grads[nets_of, :] = dot_nn(pin_net[:, of], pre_grad).astype(BF16)
    sums[...] = dot_nn(at_row[...], terms[...])
    outgoing = start_copies([(sums, sums_hbm), (net_grads, net_grads_hbm)], out_sems)
    hidden_high, hidden_low = split_bf16(sums[:, :hid])
    grad_high, grad_low = split_bf16(sums[:, hid:])
    for copy in copies:
        copy.wait()
    table_x, table_g = table[:, :feat], table[:, feat:]
    acc_in = dot_tn(table_x, grad_high) + dot_tn(table_x, grad_low)
    acc_out = dot_tn(hidden_high, table_g) + dot_tn(hidden_low, table_g)
    acc_net = dot_tn(net_feats[...], net_grads[...])
    acc_bias = jnp.broadcast_to(jnp.sum(sums[:, hid:], axis=0, keepdims=True), (8, hid))
    if fast:
        part_count, rows, _ = grads_ref.shape
        part = feat // part_count
        for to in range(part_count):
            of = slice(to * part, (to + 1) * part)
            blocks_of = [acc_in[of, :], acc_net[of, :], acc_out[of, :], acc_bias]
            grads_ref[to] = jnp.concatenate([x.astype(BF16) for x in blocks_of], axis=0)
    else:
        grads_ref[:feat, :] = acc_in
        grads_ref[feat : 2 * feat, :] = acc_net
        grads_ref[2 * feat : 2 * feat + hid, :] = acc_out
        grads_ref[2 * feat + hid :, :] = acc_bias
    for copy in outgoing:
        copy.wait()


def back_kernel(fast, pos_ref, ids_hbm, sums_hbm, net_grads_hbm, w_in_hbm, w_net_hbm, w_out_hbm, *rest):
    *outs, ids, wide, sums, net_grads, w_in_ref, w_net_ref, w_out_ref, sems, at_row, net_backs, acc = rest
    table_len = acc.shape[0]
    feat, hid = w_in_ref.shape
    blocks = net_grads.shape[0] // NETS_BLK
    pins = ids.shape[1]
    mine = pl.ds(pl.multiple_of(pos_ref[1] * hid, hid), hid)
    copies = start_copies(
        [
            (ids_hbm, ids),
            (net_grads_hbm, net_grads),
            (w_net_hbm.at[:, mine], w_net_ref),
            (w_in_hbm.at[:, mine], w_in_ref),
            (w_out_hbm.at[mine, :], w_out_ref),
            (sums_hbm, sums),
        ],
        sems,
    )
    copies[0].wait()
    columns = id_columns(ids, wide)
    rows = ids[...].astype(jnp.int32)
    for b in range(blocks):
        of = slice(b * pins, (b + 1) * pins)
        for t, tile in enumerate(tiled_rows(rows[8 + b : 9 + b, :], table_len)):
            at_row[t * 128 : (t + 1) * 128, of] = tile
    for copy in copies[1:3]:
        copy.wait()
    for b in range(blocks):
        of = slice(b * pins, (b + 1) * pins)
        nets_of = slice(b * NETS_BLK, (b + 1) * NETS_BLK)
        inverse = net_inverse(row_onehot(NETS_BLK, rows[b : b + 1, :]))
        feat_grad = (dot_nt(net_grads[nets_of, :], w_net_ref[...]) * inverse).astype(BF16)
        net_backs[of, :] = dot_nn(column_onehot(columns[:, b : b + 1], NETS_BLK), feat_grad).astype(BF16)
    for copy in copies[3:]:
        copy.wait()
    hidden_high, hidden_low = split_bf16(sums[:, :hid])
    grad_high, grad_low = split_bf16(sums[:, hid:])
    acc[:, :feat] = dot_nn(hidden_high, w_out_ref[...]) + dot_nn(hidden_low, w_out_ref[...])
    acc[:, feat:] = (
        dot_nt(grad_high, w_in_ref[...]) + dot_nt(grad_low, w_in_ref[...]) + dot_nn(at_row[...], net_backs[...])
    )
    if fast:
        own_ref, far_ref, twin_ref = outs
        length = own_ref.shape[0]
        cells = table_len - 128
        share = cells // 4
        edges = acc[cells:, :].astype(BF16)
        row = lax.broadcasted_iota(jnp.int32, (length - share, 128), 0)
        lane = lax.broadcasted_iota(jnp.int32, row.shape, 1)
        for bits, ref, at in ((0, own_ref, 0), (2, far_ref, 0), (1, twin_ref, 0), (3, twin_ref, length)):
            to = pos_ref[1] ^ bits
            rows = acc[pl.ds(pl.multiple_of(to * share, share), share), :]
            ref[at : at + share, :] = rows.astype(ref.dtype)
            of = lane == ((row >> 2) * 16 + to * 4 + (row & 3))
            ref[at + share : at + length, :] = dot_nn(of.astype(BF16), edges).astype(ref.dtype)
        return
    own_ref, send_ref = outs
    cells = own_ref.shape[0]
    own_ref[...] = acc[:cells, :]
    part_count, rows, _ = send_ref.shape
    slots = rows // 2
    for part in range(part_count):
        of = slice(cells + part * slots, cells + (part + 1) * slots)
        send_ref[part, :slots, :] = acc[of, :feat].astype(BF16)
        send_ref[part, slots:, :] = acc[of, feat:].astype(BF16)


def pair_kernel(own_ref, far_ref, twin_ref, rows_ref, edges_ref, far_rows_ref, far_edges_ref):
    length = own_ref.shape[0]
    share = rows_ref.shape[0]
    own = own_ref[...] + twin_ref[:length, :].astype(F32)
    far = far_ref[...] + twin_ref[length:, :].astype(F32)
    rows_ref[...] = own[:share]
    edges_ref[...] = own[share:]
    far_rows_ref[...] = far[:share].astype(BF16)
    far_edges_ref[...] = far[share:].astype(BF16)


def sum_kernel(got_ref, edges_ref, far_ref, *rest):
    *payloads, bias_ref = rest
    total = edges_ref[...] + far_ref[...].astype(F32)
    feat = total.shape[1] // 2
    piece = got_ref[0].astype(F32)
    for part in range(1, got_ref.shape[0]):
        piece += got_ref[part].astype(F32)
    rows = piece.shape[0] - 8
    bias_ref[...] = jnp.concatenate([piece[rows:]] * 2, axis=0).astype(BF16)
    for k, payload in enumerate(payloads):
        edges = []
        for odd in range(2):
            at = 4 * (2 * k + odd)
            edges += [total[at : at + 4, :feat], total[at : at + 4, feat:]]
        payload[...] = jnp.concatenate([piece[:rows]] + edges, axis=0).astype(BF16)


def place(pos_ref, parts, outs, buffer, sems):
    rows, hid = buffer.shape[1:]
    part = rows // 3
    copies = []
    for at, (ref, start, cell_bits, net_bits) in enumerate(parts):
        row = pl.multiple_of((pos_ref[0] ^ cell_bits) * part, part)
        first = pl.multiple_of((pos_ref[1] ^ net_bits) * hid, hid)
        buffer[at] = ref[start : start + rows, :].astype(F32)
        targets = [
            outs[0].at[pl.ds(row, part), pl.ds(first, hid)],
            outs[1].at[pl.ds(row, part), pl.ds(first, hid)],
            outs[2].at[pl.ds(pl.multiple_of(first + row, part), part), :],
        ]
        for matrix, target in enumerate(targets):
            source = buffer.at[at, matrix * part : (matrix + 1) * part, :]
            copies.append(pltpu.make_async_copy(source, target, sems.at[3 * at + matrix]))
            copies[-1].start()
    return copies


def place_kernel(tags, olds, pos_ref, *refs):
    ins, refs = refs[: len(tags)], refs[len(tags) + olds :]
    outs, (buffer, sems) = refs[:3], refs[3:]
    parts = [(ref,) + tag for ref, some in zip(ins, tags) for tag in some]
    for copy in place(pos_ref, parts, outs, buffer, sems):
        copy.wait()


def edge_rows(edges):
    return jnp.concatenate([edge[:64, :] for edge in edges], axis=0)


def first_kernel(tags, pos_ref, idx_ref, x_hbm, g_hbm, rows_ref, far_ref, *refs):
    ins, refs = refs[: len(tags)], refs[len(tags) :]
    edges, refs = refs[:2], refs[2:]
    grads, (total_ref, pick_y_ref, pick_x_ref, buffer, sems, x_ref, g_ref, row_sems) = refs[:3], refs[3:]
    share, wide = rows_ref.shape
    feat = wide // 2
    cell, net = pos_ref[0], pos_ref[1]
    mine = pl.ds(pl.multiple_of(net * share, share), share)
    copies = start_copies([(x_hbm.at[mine, :], x_ref), (g_hbm.at[mine, :], g_ref)], row_sems)
    parts = [(ref,) + tag for ref, some in zip(ins, tags) for tag in some]
    placed = place(pos_ref, parts, grads, buffer, sems)
    lane = lax.broadcasted_iota(jnp.int32, (1, 256), 1)
    bits, source, is_back, slot = lane >> 6, (lane >> 3) & 7, (lane >> 2) & 1, lane & 3
    part_of = cell ^ (((source & 3) << 1) | (source >> 2))
    ids = pick_ids(idx_ref[0], part_of, ((net ^ bits) << 2) | slot) - net * share
    pick_y = row_onehot(share, jnp.where(is_back == 0, ids, -1))
    pick_x = row_onehot(share, jnp.where(is_back == 1, ids, -1))
    pick_y_ref[...] = pick_y[:, 128:]
    pick_x_ref[...] = pick_x[:, 128:]
    halo = edge_rows(edges)
    for copy in copies:
        copy.wait()
    rows = rows_ref[...] + far_ref[...].astype(F32)
    total_ref[:, :feat] = x_ref[...].astype(F32) + rows[:, :feat] + dot_nn(pick_y[:, :128], halo)
    total_ref[:, feat:] = g_ref[...].astype(F32) + rows[:, feat:] + dot_nn(pick_x[:, :128], halo)
    for copy in placed:
        copy.wait()


def finish_kernel(tags, pos_ref, total_ref, pick_y_ref, pick_x_ref, *refs):
    ins, refs = refs[: len(tags)], refs[len(tags) :]
    edges, refs = refs[:4], refs[4 + 3 :]
    grads, (updated_ref, back_ref, bias_ref, buffer, sems) = refs[:3], refs[3:]
    feat = updated_ref.shape[1]
    parts = [(ref,) + tag for ref, some in zip(ins, tags) for tag in some]
    placed = place(pos_ref, parts, grads, buffer, sems)
    halo = edge_rows(edges[2:])
    updated_ref[...] = (total_ref[:, :feat] + dot_nn(pick_y_ref[...], halo)).astype(BF16)
    back_ref[...] = (total_ref[:, feat:] + dot_nn(pick_x_ref[...], halo)).astype(BF16)
    for bits, edge in enumerate(edges):
        at = pl.multiple_of((pos_ref[1] ^ bits) * feat, feat)
        bias_ref[:, pl.ds(at, feat)] = edge[64:, :].astype(F32)[:1]
    for copy in placed:
        copy.wait()


def combine_kernel(pos_ref, idx_ref, got_ref, own_ref, *outs):
    part_count, slots = idx_ref.shape[1:]
    cells, wide = own_ref.shape
    feat = wide // 2
    group = 128 // slots
    rows_y = own_ref[:, :feat]
    rows_x = own_ref[:, feat:]
    for first in range(0, part_count, group):
        onehot = slot_onehot(idx_ref[0, first : first + group], cells)
        y = got_ref[first : first + group, :slots, :].reshape(128, feat)
        x = got_ref[first : first + group, slots:, :].reshape(128, feat)
        rows_y += dot_nn(onehot, y)
        rows_x += dot_nn(onehot, x)
    *shares, scratch = outs
    scratch[:, :feat] = rows_y
    scratch[:, feat:] = rows_x
    share = cells // len(shares)
    for bits, share_ref in enumerate(shares):
        at = pl.multiple_of((pos_ref[1] ^ bits) * share, share)
        share_ref[...] = scratch[pl.ds(at, share), :].astype(share_ref.dtype)


def plain_rows_kernel(pos_ref, x_hbm, g_hbm, own_ref, *rest):
    *others, updated_ref, back_ref, x_ref, g_ref, sems = rest
    share, feat = updated_ref.shape
    mine = pl.ds(pl.multiple_of(pos_ref[1] * share, share), share)
    copies = start_copies([(x_hbm.at[mine, :], x_ref), (g_hbm.at[mine, :], g_ref)], sems)
    total = own_ref[...]
    for other in others:
        total += other[...].astype(F32)
    for copy in copies:
        copy.wait()
    updated_ref[...] = (x_ref[...].astype(F32) + total[:, :feat]).astype(BF16)
    back_ref[...] = (g_ref[...].astype(F32) + total[:, feat:]).astype(BF16)


def whole(count):
    return [pl.BlockSpec(memory_space=pltpu.VMEM)] * count


SMEM = pl.BlockSpec(memory_space=pltpu.SMEM)
HBM = pl.BlockSpec(memory_space=pltpu.HBM)
PARAMS = dict(compiler_params=pltpu.CompilerParams(vmem_limit_bytes=VMEM_LIMIT))


def about(microseconds):
    return pl.CostEstimate(flops=0, transcendentals=0, bytes_accessed=int(microseconds * 3.6e6))


def in_hbm(*arrays):
    return [pltpu.with_memory_space_constraint(x, pltpu.HBM) for x in arrays]


def flip(x, axis, bits):
    size = lax.axis_size(axis)
    return lax.ppermute(x, axis, [(i, i ^ bits) for i in range(size)])


def both(x, cell_bits, net_bits):
    parts, group = lax.axis_size("cell"), lax.axis_size("net")
    pairs = [
        (c * group + n, (c ^ cell_bits(n)) * group + (n ^ net_bits)) for c in range(parts) for n in range(group)
    ]
    return lax.ppermute(x, ("cell", "net"), pairs)


def local(cell_feat, out_grad, w_in, w_net, bias, w_out, send_idx, pin_net, pin_ref, block_count):
    part_count = lax.axis_size("cell")
    group_size = lax.axis_size("net")
    cells, feat = cell_feat.shape
    hidden_dim = w_in.shape[1]
    hid = hidden_dim // group_size
    slots = send_idx.shape[2]
    pins = pin_net.shape[3]
    table_len = cells + part_count * slots
    fast = part_count == 8 and group_size == 4
    pos = jnp.stack([lax.axis_index("cell"), lax.axis_index("net")]).astype(jnp.int32)

    def shape(dtype, *dims):
        return jax.ShapeDtypeStruct(dims, dtype)

    if fast:
        sent_shape = [shape(BF16, 2, slots, 2 * feat)] * 4
    else:
        sent_shape = [shape(BF16, part_count, slots, 2 * feat)]
    ints, *sent = pl.pallas_call(
        functools.partial(gather_kernel, fast),
        in_specs=whole(1) + [HBM] * 5,
        out_specs=whole(1 + len(sent_shape)),
        out_shape=[shape(jnp.int32, 1, 8, pins)] + sent_shape,
        scratch_shapes=[
            pltpu.VMEM(send_idx.shape, jnp.int32),
            pltpu.VMEM((cells, feat), BF16),
            pltpu.VMEM((cells, feat), BF16),
            pltpu.VMEM(pin_net.shape, jnp.int32),
            pltpu.VMEM(pin_ref.shape, jnp.int32),
            pltpu.SemaphoreType.DMA((5,)),
        ],
        name="take_boundary",
        cost_estimate=about(2.0),
        **PARAMS,
    )(block_count, *in_hbm(send_idx, cell_feat, out_grad, pin_net, pin_ref))
    if fast:
        all_ints = jnp.concatenate([ints, flip(ints, "net", 1)])
        all_ints = [all_ints, flip(all_ints, "net", 2)]
        near = [sent[0]] + [flip(sent[k], "cell", 2 * k) for k in (1, 2, 3)]
        cross = jnp.stack([a[1] for a in near])
    else:
        halo = [lax.all_to_all(sent[0], "cell", split_axis=0, concat_axis=0, tiled=True)]
        all_ints = [lax.all_gather(ints, "net", tiled=True)]

    blocks = group_size + 1
    part = feat // part_count
    share = cells // group_size
    edge = part_count * slots // group_size
    all_pins = blocks * pins
    spread_shape = [
        shape(BF16, all_pins, cells),
        shape(BF16, table_len, all_pins),
        shape(BF16, all_pins, NETS_BLK),
        shape(BF16, NETS_BLK, all_pins),
        shape(BF16, all_pins, table_len - cells),
        shape(BF16, feat, hid),
        shape(BF16, feat, hid),
        shape(F32, 1, hid),
        shape(BF16, hid, feat),
    ]
    ids, at_pin, *spread = pl.pallas_call(
        functools.partial(spread_kernel, fast, slots),
        in_specs=[SMEM] + whole(len(all_ints)) + [HBM] * 4,
        out_specs=[HBM] + whole(9),
        out_shape=[pltpu.HBM((16, pins), F32)] + spread_shape,
        scratch_shapes=[
            pltpu.VMEM((16, pins), F32),
            pltpu.VMEM((128, pins), F32),
            pltpu.SemaphoreType.DMA((4,)),
            pltpu.SemaphoreType.DMA,
        ],
        name="spread",
        cost_estimate=about(4.5),
        **PARAMS,
    )(pos, *all_ints, *in_hbm(w_in, w_net, bias.reshape(1, hidden_dim), w_out))
    if fast:
        cross, at_pin = lax.optimization_barrier((cross, at_pin))
        halo = near + [flip(cross, "cell", 1)]
    taken = pl.pallas_call(
        own_pins_kernel,
        in_specs=[pl.BlockSpec(memory_space=pl.ANY)] + whole(1) + [HBM] * 2,
        out_specs=whole(1)[0],
        out_shape=shape(BF16, all_pins, 2 * feat),
        scratch_shapes=[pltpu.VMEM((cells, 2 * feat), BF16), pltpu.SemaphoreType.DMA((2,))],
        name="own_pins",
        cost_estimate=about(2.5),
        **PARAMS,
    )(cross if fast else halo[0], at_pin, *in_hbm(cell_feat, out_grad))

    grads, sums, net_grads = pl.pallas_call(
        functools.partial(layer_kernel, fast, len(halo)),
        in_specs=whole(len(halo) + 9) + [HBM] * 2,
        out_specs=whole(1) + [HBM] * 2,
        out_shape=[
            shape(BF16, part_count, 3 * part + 8, feat) if fast else shape(F32, 2 * feat + hid + 8, hid),
            pltpu.HBM((table_len, 2 * hid), F32),
            pltpu.HBM((blocks * NETS_BLK, hid), BF16),
        ],
        scratch_shapes=[
            pltpu.VMEM((table_len, 2 * feat), BF16),
            pltpu.SemaphoreType.DMA((2,)),
            pltpu.VMEM((table_len, 2 * hid), F32),
            pltpu.VMEM((blocks * NETS_BLK, hid), BF16),
            pltpu.SemaphoreType.DMA((2,)),
            pltpu.VMEM((all_pins, 2 * feat), BF16),
            pltpu.VMEM((blocks * NETS_BLK, feat), BF16),
            pltpu.VMEM((all_pins, 2 * hid), BF16),
        ],
        name="layer",
        cost_estimate=about(7.7),
        **PARAMS,
    )(*halo, *spread, taken, *in_hbm(cell_feat, out_grad))

    if fast:
        got = lax.all_to_all(grads, "cell", split_axis=0, concat_axis=0, tiled=True)
        length = share + edge
        out_shape = [shape(F32, length, 2 * feat)] * 2 + [shape(BF16, 2 * length, 2 * feat)]
    else:
        out_shape = [shape(F32, cells, 2 * feat), shape(BF16, part_count, 2 * slots, feat)]
    outs = pl.pallas_call(
        functools.partial(back_kernel, fast),
        in_specs=[SMEM] + [HBM] * 6,
        out_specs=whole(len(out_shape)),
        out_shape=out_shape,
        scratch_shapes=[
            pltpu.VMEM((16, pins), F32),
            pltpu.VMEM((128, pins), F32),
            pltpu.VMEM((table_len, 2 * hid), F32),
            pltpu.VMEM((blocks * NETS_BLK, hid), BF16),
            pltpu.VMEM((feat, hid), BF16),
            pltpu.VMEM((feat, hid), BF16),
            pltpu.VMEM((hid, feat), BF16),
            pltpu.SemaphoreType.DMA((6,)),
            pltpu.VMEM((table_len, blocks * pins), BF16),
            pltpu.VMEM((blocks * pins, feat), BF16),
            pltpu.VMEM((table_len, 2 * feat), F32),
        ],
        name="back",
        cost_estimate=about(4.6),
        **PARAMS,
    )(pos, *in_hbm(ids, sums, net_grads, w_in, w_net, w_out))

    row_shapes = [shape(BF16, share, feat)] * 2
    row_scratch = [
        pltpu.VMEM((share, feat), BF16),
        pltpu.VMEM((share, feat), BF16),
        pltpu.SemaphoreType.DMA((2,)),
    ]
    grad_shapes = [shape(F32, feat, hidden_dim), shape(F32, feat, hidden_dim), shape(F32, hidden_dim, feat)]
    if not fast:
        own, send = outs
        got = lax.all_to_all(send, "cell", split_axis=0, concat_axis=0, tiled=True)
        shares = pl.pallas_call(
            combine_kernel,
            in_specs=[SMEM] + whole(3),
            out_specs=whole(group_size),
            out_shape=[shape(BF16 if bits else F32, share, 2 * feat) for bits in range(group_size)],
            scratch_shapes=[pltpu.VMEM((cells, 2 * feat), F32)],
            name="combine",
            **PARAMS,
        )(pos, send_idx, got, own)
        others = [flip(shares[bits], "net", bits) for bits in range(1, group_size)]
        updated, cell_grad = pl.pallas_call(
            plain_rows_kernel,
            in_specs=[SMEM] + [HBM] * 2 + whole(group_size),
            out_specs=whole(2),
            out_shape=row_shapes,
            scratch_shapes=row_scratch,
            name="own_rows",
            **PARAMS,
        )(pos, *in_hbm(cell_feat, out_grad), shares[0], *others)
        summed = lax.all_gather(lax.psum(grads, "cell"), "net")
        grad_in = jnp.moveaxis(summed[:, :feat], 0, 1).reshape(feat, hidden_dim)
        grad_net = jnp.moveaxis(summed[:, feat : 2 * feat], 0, 1).reshape(feat, hidden_dim)
        grad_out = summed[:, 2 * feat : 2 * feat + hid].reshape(hidden_dim, feat)
        grad_bias = summed[:, 2 * feat + hid].reshape(hidden_dim)
        return (updated, cell_grad, grad_in, grad_net, grad_bias, grad_out)

    own, far, twin_share = outs
    rows, edges, far_rows, far_edges = pl.pallas_call(
        pair_kernel,
        in_specs=whole(3),
        out_specs=whole(4),
        out_shape=[
            shape(F32, share, 2 * feat),
            shape(F32, edge, 2 * feat),
            shape(BF16, share, 2 * feat),
            shape(BF16, edge, 2 * feat),
        ],
        name="pairs",
        **PARAMS,
    )(own, far, flip(twin_share, "net", 1))
    rows_of = 3 * part
    *pays, bias_sum = pl.pallas_call(
        sum_kernel,
        in_specs=whole(3),
        out_specs=whole(5),
        out_shape=[shape(BF16, rows_of + 16, feat)] * 4 + [shape(BF16, 16, feat)],
        name="sums",
        cost_estimate=about(0.2),
        **PARAMS,
    )(got, edges, flip(far_edges, "net", 2))
    far_rows, first_pay = lax.optimization_barrier((far_rows, pays[0]))
    far_rows = flip(far_rows, "net", 2)
    pays = [first_pay] + pays[1:]
    near = [pays[0]] + [flip(pays[k], "cell", 2 * k) for k in (1, 2, 3)]
    near, far_rows = lax.optimization_barrier((near, far_rows))
    across = flip(jnp.concatenate(near[:2] + [a[rows_of:] for a in near[2:]]), "cell", 1)
    second = jnp.concatenate([a[:rows_of] for a in near[2:]])
    second = jnp.concatenate([second, flip(second, "net", 2)])
    starts = [rows_of, 2 * rows_of + 16, 2 * rows_of + 32, 2 * rows_of + 48]
    edges = [a[rows_of : rows_of + 8] for a in near] + [across[at + 8 : at + 16] for at in starts]
    full = rows_of + 16
    pieces = [near[0][:rows_of], near[1][:rows_of], across[:rows_of], across[full : full + rows_of]]
    first = jnp.concatenate(pieces + edges + [bias_sum])
    early = [flip(first, "net", 1), flip(second, "net", 1)]
    third, fourth = flip(first, "net", 2), flip(second, "cell", 1)
    first_tag = [(0, 0, 0), (rows_of, 2, 0), (2 * rows_of, 1, 0), (3 * rows_of, 3, 0)]
    second_tag = [(0, 4, 0), (rows_of, 6, 0), (2 * rows_of, 4, 2), (3 * rows_of, 6, 2)]
    early_tags = [first_tag, second_tag]
    late_tags = [[(at, c, n ^ 2) for at, c, n in first_tag], [(at, c ^ 1, n) for at, c, n in second_tag]]

    def twin(tags):
        return [[(at, c, n ^ 1) for at, c, n in tag] for tag in tags]

    def scratch(arrays):
        return [pltpu.VMEM((4 * len(arrays), rows_of, hid), F32), pltpu.SemaphoreType.DMA((12 * len(arrays),))]

    *grads, total, pick_y, pick_x = pl.pallas_call(
        functools.partial(first_kernel, early_tags + twin(early_tags)),
        in_specs=[SMEM] + whole(1) + [HBM] * 2 + whole(2 + 4 + 2),
        out_specs=[HBM] * 3 + whole(3),
        out_shape=grad_shapes + [shape(F32, share, 2 * feat)] + [shape(BF16, share, 128)] * 2,
        scratch_shapes=scratch([0] * 4) + row_scratch,
        name="first_pieces",
        **PARAMS,
    )(pos, send_idx, *in_hbm(cell_feat, out_grad), rows, far_rows, first, second, *early, first[4 * rows_of :], early[0][4 * rows_of :])
    third, fourth, grads = lax.optimization_barrier((third, fourth, grads))
    late = [flip(third, "net", 1), flip(fourth, "net", 1)]
    grads = pl.pallas_call(
        functools.partial(place_kernel, late_tags, 3),
        in_specs=[SMEM] + whole(2) + [HBM] * 3,
        out_specs=[HBM] * 3,
        out_shape=grad_shapes,
        scratch_shapes=scratch(late),
        input_output_aliases={3 + i: i for i in range(3)},
        name="place",
        **PARAMS,
    )(pos, third, fourth, *grads)
    all_edges = [a[4 * rows_of :] for a in (first, early[0], third, late[0])]
    grad_in, grad_net, grad_out, updated, cell_grad, grad_bias = pl.pallas_call(
        functools.partial(finish_kernel, twin(late_tags)),
        in_specs=[SMEM] + whole(3 + 2 + 4) + [HBM] * 3,
        out_specs=[HBM] * 3 + whole(3),
        out_shape=grad_shapes + row_shapes + [shape(F32, 1, hidden_dim)],
        scratch_shapes=scratch(late),
        input_output_aliases={4 + 2 + 4 + i: i for i in range(3)},
        name="finish",
        **PARAMS,
    )(pos, total, pick_y, pick_x, *late, *all_edges, *grads)
    return (updated, cell_grad, grad_in, grad_net, grad_bias.reshape(hidden_dim), grad_out)


def solution(mesh):
    placed = (
        P("cell", None),
        P("cell", None),
        P(),
        P(),
        P(),
        P(),
        P("cell", None, None),
        P("cell", "net", None, None),
        P("cell", "net", None, None),
        P("cell", "net"),
    )
    return jax.shard_map(
        local,
        mesh=mesh,
        in_specs=placed,
        out_specs=(P(("cell", "net"), None), P(("cell", "net"), None), P(), P(), P(), P()),
        check_vma=False,
    )
```
